512 devices in a mesh: dp: 4 (over x), ctx: 16 (over y, core), head: 8 (over z).
Axes of the slice: x: 4, y: 8, z: 8, core: 2. Of those that a mesh axis runs over, the one named last changes fastest.
Arguments:
- queries: bfloat16 [16384, 8192], P(('dp', 'ctx'), 'head'), parts along dimension 0, may hold values from -128 to 128, as said below
- keys: bfloat16 [16384, 1024], P(('dp', 'ctx'), 'head'), parts along dimension 0, may hold values from -6 to 6, as said below
- values: bfloat16 [16384, 1024], P(('dp', 'ctx'), 'head'), parts along dimension 0, may hold values from -6 to 6
- segment_ids: int32 [16384], P(('dp', 'ctx')), parts along dimension 0, may hold values from 0 to 2, never falling along the last dimension, each value on 1 to 3072 neighbouring positions
Outputs:
- attended: bfloat16 [16384, 8192], P(('dp', 'ctx'), 'head'), parts along dimension 0
The draws below stay inside these ranges and needn't reach their ends.
There are 4 independent parts, one for each index of `dp`. The reference program is written for one: setup_inputs(seed, part) draws one part's arguments, and reference() takes and returns one part's arrays. A program takes and returns all parts, laid end to end along the dimension named above; each array names one. Nothing has to cross between parts.
Inputs may be any that keep to these rules, and one draw needn't show every extreme that they name: queries: entries stay within the range. keys: entries stay within the range.
All inputs are finite; a program needn't handle non-finite values.
Results may differ from the reference program's by a relative error of at most 0.005.
Values may be sent and summed in bfloat16 or wider, within the bound.
A program may use at most 128 MiB of HBM per device.

```python
import math
import jax
import jax.numpy as jnp
import numpy as np
from jax import lax

QH = 64
KVH = 8
HD = 128
TOKENS = 4096


def shared_base(key):
    key_base = jnp.clip(jax.random.normal(jax.random.fold_in(key, 11), (TOKENS, KVH * HD), jnp.float32), -5.0, 5.0)
    query_base = jnp.clip(jax.random.normal(jax.random.fold_in(key, 12), (TOKENS, QH * HD), jnp.float32), -5.0, 5.0)
    return (key_base, query_base)


def draw_keys(key, part):
    key_base, query_base = shared_base(key)
    return key_base.astype(jnp.bfloat16)


def draw_queries(key, part):
    key_base, query_base = shared_base(key)
    return query_base.astype(jnp.bfloat16)


def shard_levels(stream_key, extent, shards, least, top_value):
    factor_of = 1.0
    for position, shards_of in shards:
        draws = jax.random.uniform(jax.random.fold_in(jax.random.fold_in(stream_key, 6), position), (shards_of,), jnp.float32, least / len(shards), top_value / len(shards))
        factor_of = factor_of * jnp.repeat(jnp.exp(draws), extent[position] // shards_of).reshape((-1,) + (1,) * (len(extent) - 1 - position))
    return factor_of


def length_profile(count, total, reach, slope):
    loads = [(1 << 20) // math.isqrt(grade ** slope) + 1 for grade in range(2, count + 1)]
    rest, given = total - reach - (count - 1), [1] * (count - 1)
    while rest > 0:
        candidates = [i for i in range(count - 1) if given[i] < reach]
        whole, left = sum([loads[i] for i in candidates]), rest
        for i in candidates:
            addition = min(reach - given[i], max(1, left * loads[i] // whole), rest)
            given[i] = given[i] + addition
            rest = rest - addition
    return np.array([reach] + given)


def ragged(rng, count, total, reach, lean):
    if count == 2:
        one = jax.random.randint(rng, (), max(1, total - reach), min(reach, total - 1) + 1)
        return jnp.stack([one, total - one])
    sizes = jnp.asarray(length_profile(count, total, reach, lean), jnp.int32)
    couples = (count - 1) // 2
    source_of, receiver = sizes[1:1 + 2 * couples:2], sizes[2:2 + 2 * couples:2]
    slack = jnp.minimum(source_of - 1, reach - receiver)
    moved = jax.random.randint(jax.random.fold_in(rng, 1), (couples,), 0, 1 << 20) % (slack + 1)
    sizes = sizes.at[1:1 + 2 * couples:2].set(source_of - moved).at[2:2 + 2 * couples:2].set(receiver + moved)
    return sizes[jax.random.permutation(jax.random.fold_in(rng, 2), count)]


def bell_draw(own_key, shape, scale, limit, cuts=(), held_as=jnp.bfloat16):
    result = jax.random.normal(own_key, shape, jnp.float32) * scale
    if len(cuts) > 0:
        result = shard_levels(own_key, shape, cuts, -0.22, 0.18) * result
    return jnp.clip(result, min=-limit, max=limit).astype(held_as)


def setup_inputs(seed: int = 0, part: int = 0) -> dict:
    key_list = jax.random.split(jax.random.key(seed), 5)
    part_keys = jax.random.split(jax.random.fold_in(key_list[4], part), 5)
    return {
        "queries": draw_queries(jax.random.fold_in(jax.random.fold_in(key_list[4], part), 71), part),
        "keys": draw_keys(jax.random.fold_in(jax.random.fold_in(key_list[4], part), 71), part),
        "values": bell_draw(part_keys[2], (TOKENS, KVH * HD), 1.0, 6.0, ((0, 16), (1, 8))),
        "segment_ids": jnp.searchsorted(jnp.cumsum(ragged(part_keys[3], 3, TOKENS, 3 * TOKENS // 4, 0)), jnp.arange(TOKENS), side="right").astype(jnp.int32),
    }


def reference(queries, keys, values, segment_ids):
    length = queries.shape[0]
    repeat = QH // KVH
    scale = HD ** -0.5
    query4 = queries.reshape(length, KVH, repeat, HD)
    key3 = keys.reshape(length, KVH, HD).astype(jnp.float32)
    value3 = values.reshape(length, KVH, HD).astype(jnp.float32)
    where_all = jnp.arange(length, dtype=jnp.int32)
    block = math.gcd(length, 128)

    def one_block(index):
        first = (index * block).astype(jnp.int32)
        query_part = lax.dynamic_slice_in_dim(query4, first, block, 0).astype(jnp.float32)
        query_pos = first + jnp.arange(block, dtype=jnp.int32)
        query_seg = lax.dynamic_slice_in_dim(segment_ids, first, block, 0)
        score = jnp.einsum('rkpd,nkd->rkpn', query_part, key3) * scale
        visible = (where_all[None, :] <= query_pos[:, None]) & (segment_ids[None, :] == query_seg[:, None])
        visible = visible[:, None, None, :]
        score = jnp.where(visible, score, -1e30)
        top = jnp.max(score, axis=-1, keepdims=True)
        weight = jnp.where(visible, jnp.exp(score - top), 0.0)
        total = jnp.sum(weight, axis=-1)
        rounded = weight.astype(jnp.bfloat16).astype(jnp.float32)
        output = jnp.einsum('rkpn,nkd->rkpd', rounded, value3) / total[..., None]
        return output.reshape(block, QH * HD).astype(jnp.bfloat16)

    blocks = lax.map(one_block, jnp.arange(length // block, dtype=jnp.int32))
    return blocks.reshape(length, QH * HD)
```

```python
import functools
import math

import jax
import jax.numpy as jnp
from jax import lax
from jax.experimental import pallas as pl
from jax.experimental.pallas import tpu as pltpu
from jax.sharding import PartitionSpec as P

HD = 128
MESH = pl.DeviceIdType.MESH
CHIPS = 8
SEG = 16
ONES = 16
HIDE = -(2.0**30)
UP, DOWN = (4, 3), (3, 4)
LAST = (2, 3)


def kernel(
    q_ref, k_ref, v_ref, seg_ref, out_ref,
    kv, qv, vv, sv, qseg, top, acc,
    in_sem, recv_sem, up_sem, down_sem, side_sem,
):
    rows = k_ref.shape[0]
    heads = q_ref.shape[1] // HD
    factor = math.log2(math.e) * HD**-0.5
    me = lax.axis_index("ctx")
    chip, core = me // 2, me % 2
    above = lax.rem(chip + 1, CHIPS) * 2 + core
    below = lax.rem(chip + CHIPS - 1, CHIPS) * 2 + core
    sibling = chip * 2 + 1 - core

    def up_comes(hop, part):
        return (chip >= hop) & (hop <= UP[part])

    def up_goes(hop, part):
        return (chip >= hop) & (hop < UP[part]) & (chip < CHIPS - 1)

    def down_comes(hop, part):
        return (lax.rem(chip + hop, CHIPS) <= LAST[part]) & (hop <= DOWN[part])

    def down_goes(hop, part):
        return (lax.rem(chip + hop, CHIPS) <= LAST[part]) & (hop < DOWN[part])

    def down_pair(hop):
        return (lax.rem(chip + hop, CHIPS) <= 2) & (chip >= 5) & (hop >= 2) & (hop <= 3)

    def down_used(hop, part):
        return down_pair(hop) | (down_comes(hop, part) & (hop == 4))

    cuts = (pl.ds(0, rows + SEG), pl.ds(rows + SEG, rows))

    def remote(block, part, send, target):
        return pltpu.make_async_remote_copy(
            src_ref=kv.at[block, cuts[part]],
            dst_ref=kv.at[block, cuts[part]],
            send_sem=send,
            recv_sem=recv_sem.at[block, part],
            device_id={"ctx": target},
            device_id_type=MESH,
        )

    def up_copy(hop, part):
        return remote((chip - hop) * 2 + core, part, up_sem.at[hop, part], above)

    def down_copy(hop, part):
        return remote(lax.rem(chip + hop, CHIPS) * 2 + core, part, down_sem.at[hop, part], below)

    def side_copy(source, part):
        return remote(source * 2 + core, part, side_sem.at[source, part], sibling)

    def arrived(block, part):
        remote(block, part, side_sem.at[0, part], sibling).wait_recv()

    barrier = pltpu.get_barrier_semaphore()

    def greet(target):
        pl.semaphore_signal(barrier, inc=1, device_id={"ctx": target}, device_id_type=MESH)

    from_below, to_above = chip >= 1, chip < CHIPS - 1
    from_above, to_below = chip != 3, chip != 4

    @pl.when(from_below)
    def _():
        greet(below)

    @pl.when(from_above)
    def _():
        greet(above)

    greet(sibling)

    k_in = pltpu.make_async_copy(k_ref, kv.at[me, pl.ds(0, rows)], in_sem.at[0])
    v_in = pltpu.make_async_copy(v_ref, vv, in_sem.at[1])
    q_in = pltpu.make_async_copy(q_ref, qv, in_sem.at[2])
    seg_in = pltpu.make_async_copy(seg_ref, sv, in_sem.at[3])
    seg_in.start()
    k_in.start()
    v_in.start()
    q_in.start()

    seg_in.wait()
    seg = sv[...]
    count = [
        jnp.sum(jnp.sum(jnp.where(seg <= d, 1.0, 0.0), axis=1, keepdims=True), axis=0, keepdims=True)
        for d in (0, 1)
    ]
    lane = lax.broadcasted_iota(jnp.int32, (8, HD), 1)
    low = jnp.where(lane == 1, count[0], jnp.where(lane == 2, count[1], 0.0))
    high = jnp.where(lane == 0, count[0], jnp.where(lane == 1, count[1], float(rows)))
    kv[me, rows : rows + SEG, :] = jnp.concatenate([low, high], axis=0).astype(jnp.bfloat16)

    def inside(low, high):
        place = lax.broadcasted_iota(jnp.int32, (rows, HD), 0).astype(jnp.float32)
        return (place >= low) & (place < high)

    lanes = lax.broadcasted_iota(jnp.int32, (rows, HD), 1)
    qseg[...] = jnp.where(inside(low[0:1], high[0:1]) & (lanes < 3), 1.0, 0.0).astype(jnp.bfloat16)

    def send_own(part):
        @pl.when(to_above)
        def _():
            up_copy(0, part).start()

        @pl.when(down_goes(0, part))
        def _():
            down_copy(0, part).start()

        @pl.when(core == 0)
        def _():
            side_copy(chip, part).start()

    k_in.wait()
    pl.semaphore_wait(barrier, to_above.astype(jnp.int32) + to_below.astype(jnp.int32) + 1)
    send_own(0)
    v_in.wait()
    turned = vv[...].astype(jnp.float32).T.astype(jnp.bfloat16)
    for half in range(rows // HD):
        at = rows + SEG + half * HD
        kv[me, at : at + HD, :] = turned[:, half * HD : (half + 1) * HD]
    send_own(1)
    q_in.wait()

    def keys_of(block):
        bounds = kv[block, rows : rows + SEG, :].astype(jnp.float32)
        hidden = jnp.where(inside(bounds[0:1], bounds[8:9]), 0.0, HIDE).astype(jnp.bfloat16)
        return jnp.concatenate([kv[block, 0:rows, :], hidden], axis=1)

    def values_of(block):
        first = rows + SEG
        return [kv[block, first + i * HD : first + (i + 1) * HD, :] for i in range(rows // HD)]

    def scores(keys, h):
        query = jnp.concatenate([qv[:, h * HD : (h + 1) * HD], qseg[...]], axis=1)
        return lax.dot_general(
            keys, query, (((1,), (1,)), ((), ())), preferred_element_type=jnp.float32
        )

    def attend(block, own=False):
        keys = keys_of(block)
        values = jnp.concatenate(values_of(block), axis=1)
        ones = jnp.ones((ONES, values.shape[1]), jnp.bfloat16)
        values = jnp.concatenate([values, ones], axis=0)

        def finish(h, weight, alpha):
            part = jnp.dot(values, weight, preferred_element_type=jnp.float32)
            acc[h] = part if own else acc[h] * alpha + part

        ahead, behind = scores(keys, 0), None
        for h in range(heads):
            score = ahead
            if h + 1 < heads:
                ahead = scores(keys, h + 1)
            if own:
                u = lax.broadcasted_iota(jnp.int32, score.shape, 0)
                t = lax.broadcasted_iota(jnp.int32, score.shape, 1)
                score = jnp.where(u <= t, score, HIDE)
            new, alpha = jnp.max(score, axis=0, keepdims=True), None
            if not own:
                old = top[h : h + 1, :]
                new = jnp.maximum(old, new)
                alpha = jnp.exp2((old - new) * factor)
            weight = jnp.exp2((score - new) * factor).astype(jnp.bfloat16)
            top[h : h + 1, :] = new
            if behind is not None:
                finish(*behind)
            behind = (h, weight, alpha)
        finish(*behind)

    attend(me, own=True)

    @pl.when(core == 1)
    def _():
        for part in range(2):
            arrived(sibling, part)
        attend(sibling)

    def one_round(hop, carry):
        above_source = lax.rem(chip + hop, CHIPS)
        for part in range(2):

            @pl.when(up_comes(hop, part))
            def _():
                arrived((chip - hop) * 2 + core, part)

                @pl.when(up_goes(hop, part))
                def _():
                    up_copy(hop, part).start()

                side_copy(chip - hop, part).start()

            @pl.when(down_comes(hop, part))
            def _():
                arrived(above_source * 2 + core, part)

                @pl.when(down_goes(hop, part))
                def _():
                    down_copy(hop, part).start()

                @pl.when(down_used(hop, part))
                def _():
                    side_copy(above_source, part).start()

        def one_block(i, carry):
            source = jnp.where(i < 2, chip - hop, above_source)
            other = i % 2

            @pl.when(other == 1)
            def _():
                for part in range(2):
                    arrived(source * 2 + 1 - core, part)

            attend(source * 2 + jnp.where(other == 1, 1 - core, core))
            return carry

        pairs = (chip >= hop).astype(jnp.int32) + down_pair(hop).astype(jnp.int32)
        return lax.fori_loop(0, 2 * pairs, one_block, carry)

    lax.fori_loop(1, 5, one_round, 0)

    for h in range(heads):
        share = acc[h, 0:HD, :] * (1.0 / acc[h, HD : HD + 1, :])
        out_ref[:, h * HD : (h + 1) * HD] = share.astype(jnp.bfloat16).T

    for part in range(2):

        @pl.when(core == 0)
        def _():
            side_copy(chip, part).wait_send()

        for hop in range(5):

            @pl.when(up_goes(hop, part))
            def _():
                up_copy(hop, part).wait_send()

            @pl.when(down_goes(hop, part))
            def _():
                down_copy(hop, part).wait_send()

        for hop in range(1, 5):

            @pl.when(up_comes(hop, part))
            def _():
                side_copy(chip - hop, part).wait_send()

            @pl.when(down_used(hop, part))
            def _():
                side_copy(lax.rem(chip + hop, CHIPS), part).wait_send()


def per_device(queries, keys, values, segment_ids):
    rows, width = queries.shape
    heads = width // HD
    size = 2 * rows + SEG
    operands = (queries, keys, values, segment_ids.reshape(rows // HD, HD))
    operands = [pltpu.with_memory_space_constraint(operand, pltpu.HBM) for operand in operands]
    return pl.pallas_call(
        kernel,
        out_shape=pltpu.VMEM((rows, width), jnp.bfloat16),
        in_specs=[pl.BlockSpec(memory_space=pltpu.HBM)] * 4,
        out_specs=pl.BlockSpec(memory_space=pltpu.VMEM),
        scratch_shapes=[
            pltpu.VMEM((2 * CHIPS, size, HD), jnp.bfloat16),
            pltpu.VMEM((rows, width), jnp.bfloat16),
            pltpu.VMEM((rows, HD), jnp.bfloat16),
            pltpu.VMEM((rows // HD, HD), jnp.int32),
            pltpu.VMEM((rows, HD), jnp.bfloat16),
            pltpu.VMEM((heads, rows), jnp.float32),
            pltpu.VMEM((heads, HD + ONES, rows), jnp.float32),
            pltpu.SemaphoreType.DMA((4,)),
            pltpu.SemaphoreType.DMA((2 * CHIPS, 2)),
            pltpu.SemaphoreType.DMA((4, 2)),
            pltpu.SemaphoreType.DMA((4, 2)),
            pltpu.SemaphoreType.DMA((CHIPS, 2)),
        ],
        compiler_params=pltpu.CompilerParams(
            collective_id=0, has_side_effects=True, vmem_limit_bytes=32 * 1024 * 1024
        ),
        cost_estimate=pl.CostEstimate(
            flops=4 * rows * rows * 13 * width,
            bytes_accessed=4 * rows * width,
            transcendentals=13 * rows * rows * heads,
        ),
        name="ring_attention",
    )(*operands)


def solution(mesh):
    in_specs = (
        P(("dp", "ctx"), "head"),
        P(("dp", "ctx"), "head"),
        P(("dp", "ctx"), "head"),
        P(("dp", "ctx")),
    )
    out_specs = P(("dp", "ctx"), "head")
    return jax.shard_map(
        per_device, mesh=mesh, in_specs=in_specs, out_specs=out_specs, check_vma=False
    )
```

```python
import functools
import math

import jax
import jax.numpy as jnp
from jax import lax
from jax.experimental import pallas as pl
from jax.experimental.pallas import tpu as pltpu
from jax.sharding import PartitionSpec as P

HD = 128
MESH = pl.DeviceIdType.MESH
CHIPS = 8
SEG = 16
ONES = 16
HIDE = -(2.0**30)
AHEAD = 2
UP, DOWN = (4, 3), (3, 4)
LAST = (2, 3)


def kernel(
    q_ref, k_ref, v_ref, seg_ref, out_ref,
    kv, qv, vv, sv, qseg, top, acc,
    in_sem, recv_sem, up_sem, down_sem, side_sem,
):
    rows = k_ref.shape[0]
    heads = q_ref.shape[1] // HD
    factor = math.log2(math.e) * HD**-0.5
    me = lax.axis_index("ctx")
    chip, core = me // 2, me % 2
    sibling = chip * 2 + 1 - core
    above_chip, below_chip = lax.rem(chip + 1, CHIPS), lax.rem(chip + CHIPS - 1, CHIPS)

    def up_comes(hop, part):
        return (chip >= hop) & (hop <= UP[part])

    def up_goes(hop, part):
        return (chip >= hop) & (hop < UP[part]) & (chip < CHIPS - 1)

    def down_passes(stream):
        return jnp.where(chip == 0, core == 1, core == stream)

    def down_comes(hop, part, stream):
        here = (lax.rem(chip + hop, CHIPS) <= LAST[part]) & (hop <= DOWN[part])
        return here & down_passes(stream)

    def down_goes(hop, part, stream):
        way = jnp.where(hop == 0, core == stream, down_passes(stream))
        return (lax.rem(chip + hop, CHIPS) <= LAST[part]) & (hop < DOWN[part]) & way

    def down_pair(hop):
        return (lax.rem(chip + hop, CHIPS) <= 2) & (chip >= 5) & (hop >= 2) & (hop <= 3)

    def down_hands(hop):
        return down_pair(hop) & ((hop == 3) | (core == 1))

    cuts = (pl.ds(0, rows + SEG), pl.ds(rows + SEG, rows))

    def remote(block, cut, send, receive, target):
        return pltpu.make_async_remote_copy(
            src_ref=kv.at[block, cut],
            dst_ref=kv.at[block, cut],
            send_sem=send,
            recv_sem=receive,
            device_id={"ctx": target},
            device_id_type=MESH,
        )

    def up_copy(hop, part):
        block = (chip - hop) * 2 + core
        send, receive = up_sem.at[hop, part], recv_sem.at[block, part]
        return remote(block, cuts[part], send, receive, above_chip * 2 + core)

    def down_copy(hop, part, stream):
        block = lax.rem(chip + hop, CHIPS) * 2 + stream
        send, receive = down_sem.at[hop, part, stream], recv_sem.at[block, part]
        target = below_chip * 2 + jnp.where(chip == 1, 1, stream)
        return remote(block, cuts[part], send, receive, target)

    whole = pl.ds(0, 2 * rows + SEG)

    def side_copy(source):
        block = source * 2 + core
        return remote(block, whole, side_sem.at[source], recv_sem.at[block, 0], sibling)

    def arrived(block, part):
        remote(block, cuts[part], up_sem.at[0, part], recv_sem.at[block, part], sibling).wait_recv()

    def handed(block):
        remote(block, whole, side_sem.at[0], recv_sem.at[block, 0], sibling).wait_recv()

    barrier = pltpu.get_barrier_semaphore()

    def greet(target):
        pl.semaphore_signal(barrier, inc=1, device_id={"ctx": target}, device_id_type=MESH)

    @pl.when(chip >= 1)
    def _():
        greet(below_chip * 2 + core)

    @pl.when((chip != 0) & (chip != 3))
    def _():
        greet(above_chip * 2 + core)

    @pl.when((chip == CHIPS - 1) & (core == 0))
    def _():
        greet(1)

    @pl.when((chip == 0) & (core == 1))
    def _():
        greet(2)
        greet(3)

    @pl.when((chip >= 1) | (core == 1))
    def _():
        greet(sibling)

    partners = [chip < CHIPS - 1, chip != 4, (chip == 0) & (core == 1), (chip >= 1) | (core == 0)]

    k_in = pltpu.make_async_copy(k_ref, kv.at[me, pl.ds(0, rows)], in_sem.at[0])
    v_in = pltpu.make_async_copy(v_ref, vv, in_sem.at[1])
    q_in = pltpu.make_async_copy(q_ref, qv, in_sem.at[2])
    seg_in = pltpu.make_async_copy(seg_ref, sv, in_sem.at[3])
    seg_in.start()
    k_in.start()
    v_in.start()
    q_in.start()

    seg_in.wait()
    seg = sv[...]
    count = [
        jnp.sum(jnp.sum(jnp.where(seg <= d, 1.0, 0.0), axis=1, keepdims=True), axis=0, keepdims=True)
        for d in (0, 1)
    ]
    lane = lax.broadcasted_iota(jnp.int32, (8, HD), 1)
    low = jnp.where(lane == 1, count[0], jnp.where(lane == 2, count[1], 0.0))
    high = jnp.where(lane == 0, count[0], jnp.where(lane == 1, count[1], float(rows)))
    kv[me, rows : rows + SEG, :] = jnp.concatenate([low, high], axis=0).astype(jnp.bfloat16)

    def inside(low, high):
        place = lax.broadcasted_iota(jnp.int32, (rows, HD), 0).astype(jnp.float32)
        return (place >= low) & (place < high)

    lanes = lax.broadcasted_iota(jnp.int32, (rows, HD), 1)
    qseg[...] = jnp.where(inside(low[0:1], high[0:1]) & (lanes < 3), 1.0, 0.0).astype(jnp.bfloat16)

    def send_own(part):
        @pl.when(chip < CHIPS - 1)
        def _():
            up_copy(0, part).start()

        for stream in range(2):

            @pl.when(down_goes(0, part, stream))
            def _():
                down_copy(0, part, stream).start()

    k_in.wait()
    pl.semaphore_wait(barrier, sum(partner.astype(jnp.int32) for partner in partners))
    send_own(0)
    v_in.wait()
    turned = vv[...].astype(jnp.float32).T.astype(jnp.bfloat16)
    for half in range(rows // HD):
        at = rows + SEG + half * HD
        kv[me, at : at + HD, :] = turned[:, half * HD : (half + 1) * HD]
    send_own(1)

    @pl.when(core == 0)
    def _():
        side_copy(chip).start()

    q_in.wait()

    def keys_of(block):
        bounds = kv[block, rows : rows + SEG, :].astype(jnp.float32)
        hidden = jnp.where(inside(bounds[0:1], bounds[8:9]), 0.0, HIDE).astype(jnp.bfloat16)
        return jnp.concatenate([kv[block, 0:rows, :], hidden], axis=1)

    def values_of(block):
        first = rows + SEG
        return [kv[block, first + i * HD : first + (i + 1) * HD, :] for i in range(rows // HD)]

    def scores(keys, h):
        query = jnp.concatenate([qv[:, h * HD : (h + 1) * HD], qseg[...]], axis=1)
        return [
            lax.dot_general(
                block, query, (((1,), (1,)), ((), ())), preferred_element_type=jnp.float32
            )
            for block in keys
        ]

    def attend(blocks, own=False):
        keys = [keys_of(block) for block in blocks]
        values = jnp.concatenate([piece for block in blocks for piece in values_of(block)], axis=1)
        ones = jnp.ones((ONES, values.shape[1]), jnp.bfloat16)
        values = jnp.concatenate([values, ones], axis=0)

        def finish(h, weight, alpha):
            part = jnp.dot(values, weight, preferred_element_type=jnp.float32)[: HD + 8]
            acc[h] = part if own else acc[h] * alpha + part

        ahead, behind = [scores(keys, h) for h in range(AHEAD)], None
        for h in range(heads):
            score = ahead.pop(0)
            if h + AHEAD < heads:
                ahead.append(scores(keys, h + AHEAD))
            if own:
                u = lax.broadcasted_iota(jnp.int32, (rows, rows), 0)
                t = lax.broadcasted_iota(jnp.int32, (rows, rows), 1)
                score = [jnp.where(u <= t, score[0], HIDE)]
            new, alpha = None, None
            for piece in score:
                most = jnp.max(piece, axis=0, keepdims=True)
                new = most if new is None else jnp.maximum(new, most)
            if not own:
                old = top[h : h + 1, :]
                new = jnp.maximum(old, new)
                alpha = jnp.exp2((old - new) * factor)
            weight = [jnp.exp2((piece - new) * factor).astype(jnp.bfloat16) for piece in score]
            top[h : h + 1, :] = new
            if behind is not None:
                finish(*behind)
            behind = (h, jnp.concatenate(weight, axis=0), alpha)
        finish(*behind)

    attend([me], own=True)

    def one_round(hop, carry):
        below_source = jnp.where(chip == 0, 0, chip - hop)
        above_source = lax.rem(chip + hop, CHIPS)
        for part in range(2):

            @pl.when((hop >= 1) & up_comes(hop, part))
            def _():
                arrived(below_source * 2 + core, part)

                @pl.when(up_goes(hop, part))
                def _():
                    up_copy(hop, part).start()

                if part == 1:
                    side_copy(below_source).start()

            for stream in range(2):

                @pl.when((hop >= 1) & down_comes(hop, part, stream))
                def _():
                    arrived(above_source * 2 + stream, part)

                    @pl.when(down_goes(hop, part, stream))
                    def _():
                        down_copy(hop, part, stream).start()

            if part == 1:

                @pl.when(down_hands(hop) | ((hop == 4) & (chip >= 4)))
                def _():
                    side_copy(above_source).start()

        pair = down_pair(hop)
        short = pair & (hop == 2) & (core == 1)
        doubles = jnp.where(short, 1, 2) * pair.astype(jnp.int32)
        alone = jnp.where(pair, 0, 2 * (chip >= hop).astype(jnp.int32))
        alone = jnp.where(short, 1, jnp.where(hop == 0, core, alone))
        alone = jnp.where(chip == 0, jnp.where(hop == 4, core, 0), alone)
        second = short | (hop == 0) | (chip == 0)

        def one_double(i, carry):
            @pl.when(i == 1)
            def _():
                handed(below_source * 2 + 1 - core)
                handed(above_source * 2 + 1 - core)

            side = jnp.where(i == 1, 1 - core, core)
            attend([below_source * 2 + side, above_source * 2 + side])
            return carry

        def one_block(i, carry):
            other = (i == 1) | second

            @pl.when(other)
            def _():
                handed(below_source * 2 + 1 - core)

            attend([below_source * 2 + jnp.where(other, 1 - core, core)])
            return carry

        lax.fori_loop(0, doubles, one_double, 0)
        lax.fori_loop(0, alone, one_block, 0)
        return carry

    lax.fori_loop(0, 5, one_round, 0)

    for h in range(heads):
        share = acc[h, 0:HD, :] * (1.0 / acc[h, HD : HD + 1, :])
        out_ref[:, h * HD : (h + 1) * HD] = share.astype(jnp.bfloat16).T

    for part in range(2):
        for hop in range(5):

            @pl.when(up_goes(hop, part))
            def _():
                up_copy(hop, part).wait_send()

            for stream in range(2):

                @pl.when(down_goes(hop, part, stream))
                def _():
                    down_copy(hop, part, stream).wait_send()

    @pl.when(core == 0)
    def _():
        side_copy(chip).wait_send()

    for hop in range(1, 5):

        @pl.when(chip >= hop)
        def _():
            side_copy(chip - hop).wait_send()

        @pl.when(down_hands(hop))
        def _():
            side_copy(lax.rem(chip + hop, CHIPS)).wait_send()


def per_device(queries, keys, values, segment_ids):
    rows, width = queries.shape
    heads = width // HD
    size = 2 * rows + SEG
    operands = (queries, keys, values, segment_ids.reshape(rows // HD, HD))
    operands = [pltpu.with_memory_space_constraint(operand, pltpu.HBM) for operand in operands]
    return pl.pallas_call(
        kernel,
        out_shape=pltpu.VMEM((rows, width), jnp.bfloat16),
        in_specs=[pl.BlockSpec(memory_space=pltpu.HBM)] * 4,
        out_specs=pl.BlockSpec(memory_space=pltpu.VMEM),
        scratch_shapes=[
            pltpu.VMEM((2 * CHIPS, size, HD), jnp.bfloat16),
            pltpu.VMEM((rows, width), jnp.bfloat16),
            pltpu.VMEM((rows, HD), jnp.bfloat16),
            pltpu.VMEM((rows // HD, HD), jnp.int32),
            pltpu.VMEM((rows, HD), jnp.bfloat16),
            pltpu.VMEM((heads, rows), jnp.float32),
            pltpu.VMEM((heads, HD + 8, rows), jnp.float32),
            pltpu.SemaphoreType.DMA((4,)),
            pltpu.SemaphoreType.DMA((2 * CHIPS, 2)),
            pltpu.SemaphoreType.DMA((4, 2)),
            pltpu.SemaphoreType.DMA((4, 2, 2)),
            pltpu.SemaphoreType.DMA((CHIPS,)),
        ],
        compiler_params=pltpu.CompilerParams(
            collective_id=0, has_side_effects=True, vmem_limit_bytes=32 * 1024 * 1024
        ),
        cost_estimate=pl.CostEstimate(
            flops=4 * rows * rows * 13 * width,
            bytes_accessed=4 * rows * width,
            transcendentals=13 * rows * rows * heads,
        ),
        name="ring_attention",
    )(*operands)


def solution(mesh):
    in_specs = (
        P(("dp", "ctx"), "head"),
        P(("dp", "ctx"), "head"),
        P(("dp", "ctx"), "head"),
        P(("dp", "ctx")),
    )
    out_specs = P(("dp", "ctx"), "head")
    return jax.shard_map(
        per_device, mesh=mesh, in_specs=in_specs, out_specs=out_specs, check_vma=False
    )
```

```python
import functools
import math

import jax
import jax.numpy as jnp
from jax import lax
from jax.experimental import pallas as pl
from jax.experimental.pallas import tpu as pltpu
from jax.sharding import PartitionSpec as P

HD = 128
MESH = pl.DeviceIdType.MESH
CHIPS = 8
SEG = 16
ONES = 16
HIDE = -(2.0**30)
AHEAD = 2
UP = (4, 3)
DOWN = 4
LAST = (2, 3)


def kernel(
    q_ref, k_ref, v_ref, seg_ref, out_ref,
    kv, qv, vv, sv, qseg, top, acc,
    in_sem, recv_sem, up_sem, down_sem, side_sem,
):
    rows = k_ref.shape[0]
    heads = q_ref.shape[1] // HD
    factor = math.log2(math.e) * HD**-0.5
    me = lax.axis_index("ctx")
    chip, core = me // 2, me % 2
    sibling = chip * 2 + 1 - core
    above_chip, below_chip = lax.rem(chip + 1, CHIPS), lax.rem(chip + CHIPS - 1, CHIPS)

    def up_comes(hop, part):
        return (chip >= hop) & ((hop <= 3) | ((hop <= UP[part]) & (chip == CHIPS - 1)))

    def up_goes(hop, part):
        return (chip >= hop) & (chip < CHIPS - 1) & ((hop < 3) | ((hop < UP[part]) & (chip == CHIPS - 2)))

    def down_passes(stream):
        return jnp.where(chip == 0, core == 1, core == stream)

    def down_comes(hop, part, stream):
        here = (lax.rem(chip + hop, CHIPS) <= LAST[part]) & (hop >= 1) & (hop <= DOWN)
        return here & ((chip < CHIPS - 1) | (hop >= 2)) & down_passes(stream)

    def down_goes(hop, part, stream):
        own = (hop == 0) & (chip <= LAST[part]) & (core == stream)
        return own | (down_comes(hop, part, stream) & (hop < DOWN))

    def down_pair(hop):
        return (lax.rem(chip + hop, CHIPS) <= 2) & (chip >= 5) & (hop >= 2) & (hop <= 3)

    def down_hands(hop, part, stream):
        pair = down_pair(hop) & ((hop == 3) | (core == 1))
        return (pair | ((hop == 4) & (chip >= 4))) & down_comes(hop, part, stream)

    cuts = (pl.ds(0, rows + SEG), pl.ds(rows + SEG, rows))

    def remote(block, part, send, target):
        return pltpu.make_async_remote_copy(
            src_ref=kv.at[block, cuts[part]],
            dst_ref=kv.at[block, cuts[part]],
            send_sem=send,
            recv_sem=recv_sem.at[block, part],
            device_id={"ctx": target},
            device_id_type=MESH,
        )

    def up_copy(hop, part):
        return remote((chip - hop) * 2 + core, part, up_sem.at[hop, part], above_chip * 2 + core)

    def down_copy(hop, part, stream):
        block = lax.rem(chip + hop, CHIPS) * 2 + stream
        target = below_chip * 2 + jnp.where(chip == 1, 1, stream)
        target = jnp.where((chip == 0) & (hop == 0), (CHIPS - 2) * 2 + stream, target)
        return remote(block, part, down_sem.at[hop, part, stream], target)

    def side_copy(source, part):
        return remote(source * 2 + core, part, side_sem.at[source, part], sibling)

    def arrived(block, part):
        remote(block, part, side_sem.at[0, part], sibling).wait_recv()

    barrier = pltpu.get_barrier_semaphore()

    def greet(target):
        pl.semaphore_signal(barrier, inc=1, device_id={"ctx": target}, device_id_type=MESH)

    @pl.when(chip >= 1)
    def _():
        greet(below_chip * 2 + core)

    @pl.when((chip >= 1) & (chip != 3) & (chip < CHIPS - 1))
    def _():
        greet(above_chip * 2 + core)

    @pl.when(chip == CHIPS - 2)
    def _():
        greet(core)

    @pl.when(chip == CHIPS - 1)
    def _():
        greet(1)

    @pl.when((chip == 0) & (core == 1))
    def _():
        greet(2)
        greet(3)

    @pl.when((chip >= 1) | (core == 1))
    def _():
        greet(sibling)

    passer = (chip == 0) & (core == 1)
    partners = [chip < CHIPS - 1, chip != 4, passer, passer, (chip >= 1) | (core == 0)]

    k_in = pltpu.make_async_copy(k_ref, kv.at[me, pl.ds(0, rows)], in_sem.at[0])
    v_in = pltpu.make_async_copy(v_ref, vv, in_sem.at[1])
    q_in = pltpu.make_async_copy(q_ref, qv, in_sem.at[2])
    seg_in = pltpu.make_async_copy(seg_ref, sv, in_sem.at[3])
    seg_in.start()
    k_in.start()
    v_in.start()
    q_in.start()

    seg_in.wait()
    seg = sv[...]
    count = [
        jnp.sum(jnp.sum(jnp.where(seg <= d, 1.0, 0.0), axis=1, keepdims=True), axis=0, keepdims=True)
        for d in (0, 1)
    ]
    lane = lax.broadcasted_iota(jnp.int32, (8, HD), 1)
    low = jnp.where(lane == 1, count[0], jnp.where(lane == 2, count[1], 0.0))
    high = jnp.where(lane == 0, count[0], jnp.where(lane == 1, count[1], float(rows)))
    kv[me, rows : rows + SEG, :] = jnp.concatenate([low, high], axis=0).astype(jnp.bfloat16)

    def inside(low, high):
        place = lax.broadcasted_iota(jnp.int32, (rows, HD), 0).astype(jnp.float32)
        return (place >= low) & (place < high)

    lanes = lax.broadcasted_iota(jnp.int32, (rows, HD), 1)
    qseg[...] = jnp.where(inside(low[0:1], high[0:1]) & (lanes < 3), 1.0, 0.0).astype(jnp.bfloat16)

    def send_own(part):
        @pl.when(chip < CHIPS - 1)
        def _():
            up_copy(0, part).start()

        for stream in range(2):

            @pl.when((core == stream) & (chip <= LAST[part]))
            def _():
                down_copy(0, part, stream).start()

        @pl.when(core == 0)
        def _():
            side_copy(chip, part).start()

    k_in.wait()
    pl.semaphore_wait(barrier, sum(partner.astype(jnp.int32) for partner in partners))
    send_own(0)
    v_in.wait()
    turned = vv[...].astype(jnp.float32).T.astype(jnp.bfloat16)
    for half in range(rows // HD):
        at = rows + SEG + half * HD
        kv[me, at : at + HD, :] = turned[:, half * HD : (half + 1) * HD]
    send_own(1)
    q_in.wait()

    def keys_of(block):
        bounds = kv[block, rows : rows + SEG, :].astype(jnp.float32)
        hidden = jnp.where(inside(bounds[0:1], bounds[8:9]), 0.0, HIDE).astype(jnp.bfloat16)
        return jnp.concatenate([kv[block, 0:rows, :], hidden], axis=1)

    def values_of(block):
        first = rows + SEG
        return [kv[block, first + i * HD : first + (i + 1) * HD, :] for i in range(rows // HD)]

    def scores(keys, h):
        query = jnp.concatenate([qv[:, h * HD : (h + 1) * HD], qseg[...]], axis=1)
        return [
            lax.dot_general(
                block, query, (((1,), (1,)), ((), ())), preferred_element_type=jnp.float32
            )
            for block in keys
        ]

    def attend(blocks, own=False):
        keys = [keys_of(block) for block in blocks]
        values = jnp.concatenate([piece for block in blocks for piece in values_of(block)], axis=1)
        ones = jnp.ones((ONES, values.shape[1]), jnp.bfloat16)
        values = jnp.concatenate([values, ones], axis=0)

        def finish(h, weight, alpha):
            part = jnp.dot(values, weight, preferred_element_type=jnp.float32)[: HD + 8]
            acc[h] = part if own else acc[h] * alpha + part

        ahead, behind = [scores(keys, h) for h in range(AHEAD)], None
        for h in range(heads):
            score = ahead.pop(0)
            if h + AHEAD < heads:
                ahead.append(scores(keys, h + AHEAD))
            if own:
                u = lax.broadcasted_iota(jnp.int32, (rows, rows), 0)
                t = lax.broadcasted_iota(jnp.int32, (rows, rows), 1)
                score = [jnp.where(u <= t, score[0], HIDE)]
            new, alpha = None, None
            for piece in score:
                most = jnp.max(piece, axis=0, keepdims=True)
                new = most if new is None else jnp.maximum(new, most)
            if not own:
                old = top[h : h + 1, :]
                new = jnp.maximum(old, new)
                alpha = jnp.exp2((old - new) * factor)
            weight = [jnp.exp2((piece - new) * factor).astype(jnp.bfloat16) for piece in score]
            top[h : h + 1, :] = new
            if behind is not None:
                finish(*behind)
            behind = (h, jnp.concatenate(weight, axis=0), alpha)
        finish(*behind)

    attend([me], own=True)

    def one_round(hop, carry):
        below_source = jnp.where(chip == 0, 0, chip - hop)
        above_source = lax.rem(chip + hop, CHIPS)

        def relay_up(part):
            @pl.when((hop >= 1) & up_comes(hop, part))
            def _():
                arrived(below_source * 2 + core, part)

                @pl.when(up_goes(hop, part))
                def _():
                    up_copy(hop, part).start()

                side_copy(below_source, part).start()

        def relay_down(part, stream, turn):
            @pl.when(turn & down_comes(hop, part, stream))
            def _():
                arrived(above_source * 2 + stream, part)

                @pl.when(down_goes(hop, part, stream))
                def _():
                    down_copy(hop, part, stream).start()

                @pl.when(down_hands(hop, part, stream))
                def _():
                    side_copy(above_source, part).start()

        first = (chip == 1) | (chip == CHIPS - 1)
        for part in range(2):
            for stream in range(2):
                relay_down(part, stream, first)
            relay_up(part)
            for stream in range(2):
                relay_down(part, stream, jnp.logical_not(first))

        def handed(block):
            for part in range(2):
                arrived(block, part)

        pair = down_pair(hop)
        short = pair & (hop == 2) & (core == 1)
        doubles = jnp.where(short, 1, 2) * pair.astype(jnp.int32)
        alone = jnp.where(pair, 0, 2 * (chip >= hop).astype(jnp.int32))
        alone = jnp.where(short, 1, jnp.where(hop == 0, core, alone))
        alone = jnp.where(chip == 0, jnp.where(hop == 4, core, 0), alone)
        second = short | (hop == 0) | (chip == 0)

        def one_double(i, carry):
            @pl.when(i == 1)
            def _():
                handed(below_source * 2 + 1 - core)
                handed(above_source * 2 + 1 - core)

            side = jnp.where(i == 1, 1 - core, core)
            attend([below_source * 2 + side, above_source * 2 + side])
            return carry

        def one_block(i, carry):
            other = (i == 1) | second

            @pl.when(other)
            def _():
                handed(below_source * 2 + 1 - core)

            attend([below_source * 2 + jnp.where(other, 1 - core, core)])
            return carry

        lax.fori_loop(0, doubles, one_double, 0)
        lax.fori_loop(0, alone, one_block, 0)
        return carry

    lax.fori_loop(0, 5, one_round, 0)

    for h in range(heads):
        share = acc[h, 0:HD, :] * (1.0 / acc[h, HD : HD + 1, :])
        out_ref[:, h * HD : (h + 1) * HD] = share.astype(jnp.bfloat16).T

    for part in range(2):

        @pl.when(core == 0)
        def _():
            side_copy(chip, part).wait_send()

        for hop in range(4):

            @pl.when(up_goes(hop, part))
            def _():
                up_copy(hop, part).wait_send()

            for stream in range(2):

                @pl.when(down_goes(hop, part, stream))
                def _():
                    down_copy(hop, part, stream).wait_send()

        for hop in range(1, 5):

            @pl.when(up_comes(hop, part))
            def _():
                side_copy(chip - hop, part).wait_send()

            for stream in range(2):

                @pl.when(down_hands(hop, part, stream))
                def _():
                    side_copy(lax.rem(chip + hop, CHIPS), part).wait_send()


def per_device(queries, keys, values, segment_ids):
    rows, width = queries.shape
    heads = width // HD
    size = 2 * rows + SEG
    operands = (queries, keys, values, segment_ids.reshape(rows // HD, HD))
    operands = [pltpu.with_memory_space_constraint(operand, pltpu.HBM) for operand in operands]
    return pl.pallas_call(
        kernel,
        out_shape=pltpu.VMEM((rows, width), jnp.bfloat16),
        in_specs=[pl.BlockSpec(memory_space=pltpu.HBM)] * 4,
        out_specs=pl.BlockSpec(memory_space=pltpu.VMEM),
        scratch_shapes=[
            pltpu.VMEM((2 * CHIPS, size, HD), jnp.bfloat16),
            pltpu.VMEM((rows, width), jnp.bfloat16),
            pltpu.VMEM((rows, HD), jnp.bfloat16),
            pltpu.VMEM((rows // HD, HD), jnp.int32),
            pltpu.VMEM((rows, HD), jnp.bfloat16),
            pltpu.VMEM((heads, rows), jnp.float32),
            pltpu.VMEM((heads, HD + 8, rows), jnp.float32),
            pltpu.SemaphoreType.DMA((4,)),
            pltpu.SemaphoreType.DMA((2 * CHIPS, 2)),
            pltpu.SemaphoreType.DMA((4, 2)),
            pltpu.SemaphoreType.DMA((4, 2, 2)),
            pltpu.SemaphoreType.DMA((CHIPS, 2)),
        ],
        compiler_params=pltpu.CompilerParams(
            collective_id=0, has_side_effects=True, vmem_limit_bytes=32 * 1024 * 1024
        ),
        cost_estimate=pl.CostEstimate(
            flops=4 * rows * rows * 13 * width,
            bytes_accessed=4 * rows * width,
            transcendentals=13 * rows * rows * heads,
        ),
        name="ring_attention",
    )(*operands)


def solution(mesh):
    in_specs = (
        P(("dp", "ctx"), "head"),
        P(("dp", "ctx"), "head"),
        P(("dp", "ctx"), "head"),
        P(("dp", "ctx")),
    )
    out_specs = P(("dp", "ctx"), "head")
    return jax.shard_map(
        per_device, mesh=mesh, in_specs=in_specs, out_specs=out_specs, check_vma=False
    )
```

```python
import functools
import math

import jax
import jax.numpy as jnp
from jax import lax
from jax.experimental import pallas as pl
from jax.experimental.pallas import tpu as pltpu
from jax.sharding import PartitionSpec as P

HD = 128
MESH = pl.DeviceIdType.MESH
CHIPS = 8
SEG = 16
ONES = 16
HIDE = -(2.0**30)
AHEAD = 2
PLAN = (
    ("d1K", "d1V", "d2K", "d2V", "d3V", "C0"),
    ("C0", "d1K", "u1K", "d1V", "u1V", "a1", "d2V", "b1"),
    ("C0", "u1K", "d1V", "u1V", "a1", "u2K", "b1", "u2V", "a2", "b2"),
    (
        "C0", "u1K", "u1V", "a1", "u2K", "b1", "u2V", "a2", "u3K", "b2", "u3V", "a3",
        "b3",
    ),
    (
        "C0", "u1K", "u1V", "a1", "b1", "u2K", "d4K", "u2V", "a2", "d4V", "b2", "A4",
        "u3K", "B4", "u3V", "a3", "b3",
    ),
    (
        "C0", "u1K", "d3K", "u1V", "a1", "d3V", "b1", "u2K", "A3", "u2V", "a2", "B3",
        "b2", "u3K", "d4K", "u3V", "a3", "d4V", "A4", "b3", "B4",
    ),
    (
        "C0", "d2K", "u1K", "d2V", "u1V", "a1", "A2", "u2K", "b1", "d3K", "B2", "u2V",
        "a2", "d3V", "A3", "u3K", "b2", "d4K", "u3V", "a3", "B3", "d4V", "A4", "b3",
        "B4",
    ),
    (
        "C0", "u1K", "u1V", "a1", "d2K", "b1", "u2K", "d2V", "A2", "u2V", "a2", "d3K",
        "B2", "u3K", "b2", "d3V", "A3", "u3V", "a3", "B3", "d4V", "b3", "u4K", "a4",
        "b4",
    ),
)
KINDS = "udabABC"
DIGITS = 5


def word_of(steps):
    word = 0
    for place, step in enumerate(steps):
        rank = 8 * KINDS.index(step[0]) + 2 * max(int(step[1]) - 1, 0) + step.endswith("V")
        word += (rank + 1) << (6 * place)
    return word

UP = (4, 3)
DOWN = 4
LAST = (2, 3)


def kernel(
    q_ref, k_ref, v_ref, seg_ref, out_ref,
    kv, qv, vv, sv, qseg, top, acc,
    in_sem, recv_sem, up_sem, down_sem, side_sem,
):
    rows = k_ref.shape[0]
    heads = q_ref.shape[1] // HD
    factor = math.log2(math.e) * HD**-0.5
    me = lax.axis_index("ctx")
    chip, core = me // 2, me % 2
    sibling = chip * 2 + 1 - core
    above_chip, below_chip = lax.rem(chip + 1, CHIPS), lax.rem(chip + CHIPS - 1, CHIPS)

    def up_comes(hop, part):
        return (chip >= hop) & ((hop <= 3) | ((hop <= UP[part]) & (chip == CHIPS - 1)))

    def up_goes(hop, part):
        return (chip >= hop) & (chip < CHIPS - 1) & ((hop < 3) | ((hop < UP[part]) & (chip == CHIPS - 2)))

    def down_passes(stream):
        return jnp.where(chip == 0, core == 1, core == stream)

    def down_comes(hop, part, stream):
        here = (lax.rem(chip + hop, CHIPS) <= LAST[part]) & (hop >= 1) & (hop <= DOWN)
        return here & ((chip < CHIPS - 1) | (hop >= 2)) & down_passes(stream)

    def down_goes(hop, part, stream):
        own = (hop == 0) & (chip <= LAST[part]) & (core == stream)
        return own | (down_comes(hop, part, stream) & (hop < DOWN))

    def down_pair(hop):
        return (lax.rem(chip + hop, CHIPS) <= 2) & (chip >= 5) & (hop >= 2) & (hop <= 3)

    def down_hands(hop, part, stream):
        pair = down_pair(hop) & ((hop == 3) | (core == 1))
        return (pair | ((hop == 4) & (chip >= 4))) & down_comes(hop, part, stream)

    cuts = (pl.ds(0, rows + SEG), pl.ds(rows + SEG, rows))

    def remote(block, part, send, target):
        return pltpu.make_async_remote_copy(
            src_ref=kv.at[block, cuts[part]],
            dst_ref=kv.at[block, cuts[part]],
            send_sem=send,
            recv_sem=recv_sem.at[block, part],
            device_id={"ctx": target},
            device_id_type=MESH,
        )

    def up_copy(hop, part):
        return remote((chip - hop) * 2 + core, part, up_sem.at[hop, part], above_chip * 2 + core)

    def down_copy(hop, part, stream):
        block = lax.rem(chip + hop, CHIPS) * 2 + stream
        target = below_chip * 2 + jnp.where(chip == 1, 1, stream)
        target = jnp.where((chip == 0) & (hop == 0), (CHIPS - 2) * 2 + stream, target)
        return remote(block, part, down_sem.at[hop, part, stream], target)

    def side_copy(source, part):
        return remote(source * 2 + core, part, side_sem.at[source, part], sibling)

    def arrived(block, part):
        remote(block, part, side_sem.at[0, part], sibling).wait_recv()

    barrier = pltpu.get_barrier_semaphore()

    def greet(target):
        pl.semaphore_signal(barrier, inc=1, device_id={"ctx": target}, device_id_type=MESH)

    @pl.when(chip >= 1)
    def _():
        greet(below_chip * 2 + core)

    @pl.when((chip >= 1) & (chip != 3) & (chip < CHIPS - 1))
    def _():
        greet(above_chip * 2 + core)

    @pl.when(chip == CHIPS - 2)
    def _():
        greet(core)

    @pl.when(chip == CHIPS - 1)
    def _():
        greet(1)

    @pl.when((chip == 0) & (core == 1))
    def _():
        greet(2)
        greet(3)

    @pl.when((chip >= 1) | (core == 1))
    def _():
        greet(sibling)

    passer = (chip == 0) & (core == 1)
    partners = [chip < CHIPS - 1, chip != 4, passer, passer, (chip >= 1) | (core == 0)]

    k_in = pltpu.make_async_copy(k_ref, kv.at[me, pl.ds(0, rows)], in_sem.at[0])
    v_in = pltpu.make_async_copy(v_ref, vv, in_sem.at[1])
    q_in = pltpu.make_async_copy(q_ref, qv, in_sem.at[2])
    seg_in = pltpu.make_async_copy(seg_ref, sv, in_sem.at[3])
    seg_in.start()
    k_in.start()
    v_in.start()
    q_in.start()

    seg_in.wait()
    seg = sv[...]
    count = [
        jnp.sum(jnp.sum(jnp.where(seg <= d, 1.0, 0.0), axis=1, keepdims=True), axis=0, keepdims=True)
        for d in (0, 1)
    ]
    lane = lax.broadcasted_iota(jnp.int32, (8, HD), 1)
    low = jnp.where(lane == 1, count[0], jnp.where(lane == 2, count[1], 0.0))
    high = jnp.where(lane == 0, count[0], jnp.where(lane == 1, count[1], float(rows)))
    kv[me, rows : rows + SEG, :] = jnp.concatenate([low, high], axis=0).astype(jnp.bfloat16)

    def inside(low, high):
        place = lax.broadcasted_iota(jnp.int32, (rows, HD), 0).astype(jnp.float32)
        return (place >= low) & (place < high)

    lanes = lax.broadcasted_iota(jnp.int32, (rows, HD), 1)
    qseg[...] = jnp.where(inside(low[0:1], high[0:1]) & (lanes < 3), 1.0, 0.0).astype(jnp.bfloat16)

    def send_own(part):
        @pl.when(chip < CHIPS - 1)
        def _():
            up_copy(0, part).start()

        for stream in range(2):

            @pl.when((core == stream) & (chip <= LAST[part]))
            def _():
                down_copy(0, part, stream).start()

        @pl.when(core == 0)
        def _():
            side_copy(chip, part).start()

    k_in.wait()
    pl.semaphore_wait(barrier, sum(partner.astype(jnp.int32) for partner in partners))
    send_own(0)
    v_in.wait()
    turned = vv[...].astype(jnp.float32).T.astype(jnp.bfloat16)
    for half in range(rows // HD):
        at = rows + SEG + half * HD
        kv[me, at : at + HD, :] = turned[:, half * HD : (half + 1) * HD]
    send_own(1)
    q_in.wait()

    def keys_of(block):
        bounds = kv[block, rows : rows + SEG, :].astype(jnp.float32)
        hidden = jnp.where(inside(bounds[0:1], bounds[8:9]), 0.0, HIDE).astype(jnp.bfloat16)
        return jnp.concatenate([kv[block, 0:rows, :], hidden], axis=1)

    def values_of(block):
        first = rows + SEG
        return [kv[block, first + i * HD : first + (i + 1) * HD, :] for i in range(rows // HD)]

    def scores(keys, h):
        query = jnp.concatenate([qv[:, h * HD : (h + 1) * HD], qseg[...]], axis=1)
        return [
            lax.dot_general(
                block, query, (((1,), (1,)), ((), ())), preferred_element_type=jnp.float32
            )
            for block in keys
        ]

    def attend(blocks, own=False):
        keys = [keys_of(block) for block in blocks]
        values = jnp.concatenate([piece for block in blocks for piece in values_of(block)], axis=1)
        ones = jnp.ones((ONES, values.shape[1]), jnp.bfloat16)
        values = jnp.concatenate([values, ones], axis=0)

        def finish(h, weight, alpha):
            part = jnp.dot(values, weight, preferred_element_type=jnp.float32)[: HD + 8]
            acc[h] = part if own else acc[h] * alpha + part

        ahead, behind = [scores(keys, h) for h in range(AHEAD)], None
        for h in range(heads):
            score = ahead.pop(0)
            if h + AHEAD < heads:
                ahead.append(scores(keys, h + AHEAD))
            if own:
                u = lax.broadcasted_iota(jnp.int32, (rows, rows), 0)
                t = lax.broadcasted_iota(jnp.int32, (rows, rows), 1)
                score = [jnp.where(u <= t, score[0], HIDE)]
            new, alpha = None, None
            for piece in score:
                most = jnp.max(piece, axis=0, keepdims=True)
                new = most if new is None else jnp.maximum(new, most)
            if not own:
                old = top[h : h + 1, :]
                new = jnp.maximum(old, new)
                alpha = jnp.exp2((old - new) * factor)
            weight = [jnp.exp2((piece - new) * factor).astype(jnp.bfloat16) for piece in score]
            top[h : h + 1, :] = new
            if behind is not None:
                finish(*behind)
            behind = (h, jnp.concatenate(weight, axis=0), alpha)
        finish(*behind)

    attend([me], own=True)

    def relay_up(hop, part):
        source = chip - hop
        arrived(source * 2 + core, part)

        @pl.when(up_goes(hop, part))
        def _():
            up_copy(hop, part).start()

        side_copy(source, part).start()

    def relay_down(hop, part, stream):
        @pl.when(down_comes(hop, part, stream))
        def _():
            source = lax.rem(chip + hop, CHIPS)
            arrived(source * 2 + stream, part)

            @pl.when(down_goes(hop, part, stream))
            def _():
                down_copy(hop, part, stream).start()

            @pl.when(down_hands(hop, part, stream))
            def _():
                side_copy(source, part).start()

    def use(kind, hop):
        other = (kind == 4) | (kind == 6) | (kind == 7)
        source = jnp.where(kind <= 4, chip - hop, lax.rem(chip + hop, CHIPS))
        source = jnp.where(kind == 7, chip, source)
        unseen = other & (core == 1) & (chip - source == 6)
        unseen = unseen | ((kind == 7) & (core == 0))

        @pl.when(jnp.logical_not(unseen))
        def _():
            @pl.when(other)
            def _():
                for part in range(2):
                    arrived(source * 2 + 1 - core, part)

            attend([source * 2 + jnp.where(other, 1 - core, core)])

    def one_step(_, word):
        rank = lax.rem(word, 64) + 7
        kind, rest = lax.div(rank, 8), lax.rem(rank, 8)
        hop, value = lax.div(rest, 2) + 1, lax.rem(rest, 2)

        @pl.when(kind == 1)
        def _():
            for part in range(2):

                @pl.when(value == part)
                def _():
                    relay_up(hop, part)

        @pl.when(kind == 2)
        def _():
            for part in range(2):

                @pl.when(value == part)
                def _():
                    for stream in range(2):
                        relay_down(hop, part, stream)

        @pl.when(kind >= 3)
        def _():
            use(kind, hop)

        return lax.div(word, 64)

    words = []
    for first in range(0, max(len(steps) for steps in PLAN), DIGITS):
        word = jnp.int32(0)
        for place, steps in enumerate(PLAN):
            word = jnp.where(chip == place, word_of(steps[first : first + DIGITS]), word)
        words.append(word)

    def one_word(i, carry):
        word = words[0]
        for place in range(1, len(words)):
            word = jnp.where(i == place, words[place], word)
        lax.fori_loop(0, DIGITS, one_step, word)
        return carry

    lax.fori_loop(0, len(words), one_word, 0)

    for h in range(heads):
        share = acc[h, 0:HD, :] * (1.0 / acc[h, HD : HD + 1, :])
        out_ref[:, h * HD : (h + 1) * HD] = share.astype(jnp.bfloat16).T

    for part in range(2):

        @pl.when(core == 0)
        def _():
            side_copy(chip, part).wait_send()

        for hop in range(4):

            @pl.when(up_goes(hop, part))
            def _():
                up_copy(hop, part).wait_send()

            for stream in range(2):

                @pl.when(down_goes(hop, part, stream))
                def _():
                    down_copy(hop, part, stream).wait_send()

        for hop in range(1, 5):

            @pl.when(up_comes(hop, part))
            def _():
                side_copy(chip - hop, part).wait_send()

            for stream in range(2):

                @pl.when(down_hands(hop, part, stream))
                def _():
                    side_copy(lax.rem(chip + hop, CHIPS), part).wait_send()


def per_device(queries, keys, values, segment_ids):
    rows, width = queries.shape
    heads = width // HD
    size = 2 * rows + SEG
    operands = (queries, keys, values, segment_ids.reshape(rows // HD, HD))
    operands = [pltpu.with_memory_space_constraint(operand, pltpu.HBM) for operand in operands]
    return pl.pallas_call(
        kernel,
        out_shape=pltpu.VMEM((rows, width), jnp.bfloat16),
        in_specs=[pl.BlockSpec(memory_space=pltpu.HBM)] * 4,
        out_specs=pl.BlockSpec(memory_space=pltpu.VMEM),
        scratch_shapes=[
            pltpu.VMEM((2 * CHIPS, size, HD), jnp.bfloat16),
            pltpu.VMEM((rows, width), jnp.bfloat16),
            pltpu.VMEM((rows, HD), jnp.bfloat16),
            pltpu.VMEM((rows // HD, HD), jnp.int32),
            pltpu.VMEM((rows, HD), jnp.bfloat16),
            pltpu.VMEM((heads, rows), jnp.float32),
            pltpu.VMEM((heads, HD + 8, rows), jnp.float32),
            pltpu.SemaphoreType.DMA((4,)),
            pltpu.SemaphoreType.DMA((2 * CHIPS, 2)),
            pltpu.SemaphoreType.DMA((4, 2)),
            pltpu.SemaphoreType.DMA((4, 2, 2)),
            pltpu.SemaphoreType.DMA((CHIPS, 2)),
        ],
        compiler_params=pltpu.CompilerParams(
            collective_id=0, has_side_effects=True, vmem_limit_bytes=32 * 1024 * 1024
        ),
        cost_estimate=pl.CostEstimate(
            flops=4 * rows * rows * 13 * width,
            bytes_accessed=4 * rows * width,
            transcendentals=13 * rows * rows * heads,
        ),
        name="ring_attention",
    )(*operands)


def solution(mesh):
    in_specs = (
        P(("dp", "ctx"), "head"),
        P(("dp", "ctx"), "head"),
        P(("dp", "ctx"), "head"),
        P(("dp", "ctx")),
    )
    out_specs = P(("dp", "ctx"), "head")
    return jax.shard_map(
        per_device, mesh=mesh, in_specs=in_specs, out_specs=out_specs, check_vma=False
    )
```

```python
import functools
import math

import jax
import jax.numpy as jnp
from jax import lax
from jax.experimental import pallas as pl
from jax.experimental.pallas import tpu as pltpu
from jax.sharding import PartitionSpec as P

HD = 128
MESH = pl.DeviceIdType.MESH
CHIPS = 8
SEG = 16
ONES = 16
HIDE = -(2.0**30)
AHEAD = 2
UP = (4, 3)
DOWN = 4
LAST = (2, 3)


def kernel(
    q_ref, k_ref, v_ref, seg_ref, out_ref,
    kv, qv, vv, sv, qseg, top, acc,
    in_sem, recv_sem, up_sem, down_sem, side_sem,
):
    rows = k_ref.shape[0]
    heads = q_ref.shape[1] // HD
    factor = math.log2(math.e) * HD**-0.5
    me = lax.axis_index("ctx")
    chip, core = me // 2, me % 2
    sibling = chip * 2 + 1 - core
    above_chip, below_chip = lax.rem(chip + 1, CHIPS), lax.rem(chip + CHIPS - 1, CHIPS)

    def up_comes(hop, part):
        return (chip >= hop) & ((hop <= 3) | ((hop <= UP[part]) & (chip == CHIPS - 1)))

    def up_goes(hop, part):
        return (chip >= hop) & (chip < CHIPS - 1) & ((hop < 3) | ((hop < UP[part]) & (chip == CHIPS - 2)))

    def down_passes(stream):
        return jnp.where(chip == 0, core == 1, core == stream)

    def down_comes(hop, part, stream):
        here = (lax.rem(chip + hop, CHIPS) <= LAST[part]) & (hop >= 1) & (hop <= DOWN)
        return here & ((chip < CHIPS - 1) | (hop >= 2)) & down_passes(stream)

    def down_goes(hop, part, stream):
        own = (hop == 0) & (chip <= LAST[part]) & (core == stream)
        return own | (down_comes(hop, part, stream) & (hop < DOWN))

    def down_pair(hop):
        return (lax.rem(chip + hop, CHIPS) <= 2) & (chip >= 5) & (hop >= 2) & (hop <= 3)

    def down_hands(hop, part, stream):
        pair = down_pair(hop) & ((hop == 3) | (core == 1))
        return (pair | ((hop == 4) & (chip >= 4))) & down_comes(hop, part, stream)

    cuts = (pl.ds(0, rows + SEG), pl.ds(rows + SEG, rows))

    def remote(block, part, send, target):
        return pltpu.make_async_remote_copy(
            src_ref=kv.at[block, cuts[part]],
            dst_ref=kv.at[block, cuts[part]],
            send_sem=send,
            recv_sem=recv_sem.at[block, part],
            device_id={"ctx": target},
            device_id_type=MESH,
        )

    def up_copy(hop, part):
        return remote((chip - hop) * 2 + core, part, up_sem.at[hop, part], above_chip * 2 + core)

    def down_copy(hop, part, stream):
        block = lax.rem(chip + hop, CHIPS) * 2 + stream
        target = below_chip * 2 + jnp.where(chip == 1, 1, stream)
        target = jnp.where((chip == 0) & (hop == 0), (CHIPS - 2) * 2 + stream, target)
        return remote(block, part, down_sem.at[hop, part, stream], target)

    def side_copy(source, part):
        return remote(source * 2 + core, part, side_sem.at[source, part], sibling)

    def arrived(block, part):
        remote(block, part, side_sem.at[0, part], sibling).wait_recv()

    barrier = pltpu.get_barrier_semaphore()

    def greet(target):
        pl.semaphore_signal(barrier, inc=1, device_id={"ctx": target}, device_id_type=MESH)

    @pl.when(chip >= 1)
    def _():
        greet(below_chip * 2 + core)

    @pl.when((chip >= 1) & (chip != 3) & (chip < CHIPS - 1))
    def _():
        greet(above_chip * 2 + core)

    @pl.when(chip == CHIPS - 2)
    def _():
        greet(core)

    @pl.when(chip == CHIPS - 1)
    def _():
        greet(1)

    @pl.when((chip == 0) & (core == 1))
    def _():
        greet(2)
        greet(3)

    @pl.when((chip >= 1) | (core == 1))
    def _():
        greet(sibling)

    passer = (chip == 0) & (core == 1)
    partners = [chip < CHIPS - 1, chip != 4, passer, passer, (chip >= 1) | (core == 0)]

    k_in = pltpu.make_async_copy(k_ref, kv.at[me, pl.ds(0, rows)], in_sem.at[0])
    v_in = pltpu.make_async_copy(v_ref, vv, in_sem.at[1])
    q_in = pltpu.make_async_copy(q_ref, qv, in_sem.at[2])
    seg_in = pltpu.make_async_copy(seg_ref, sv, in_sem.at[3])
    seg_in.start()
    k_in.start()
    v_in.start()
    q_in.start()

    seg_in.wait()
    seg = sv[...]
    count = [
        jnp.sum(jnp.sum(jnp.where(seg <= d, 1.0, 0.0), axis=1, keepdims=True), axis=0, keepdims=True)
        for d in (0, 1)
    ]
    lane = lax.broadcasted_iota(jnp.int32, (8, HD), 1)
    low = jnp.where(lane == 1, count[0], jnp.where(lane == 2, count[1], 0.0))
    high = jnp.where(lane == 0, count[0], jnp.where(lane == 1, count[1], float(rows)))
    kv[me, rows : rows + SEG, :] = jnp.concatenate([low, high], axis=0).astype(jnp.bfloat16)

    def inside(low, high):
        place = lax.broadcasted_iota(jnp.int32, (rows, HD), 0).astype(jnp.float32)
        return (place >= low) & (place < high)

    lanes = lax.broadcasted_iota(jnp.int32, (rows, HD), 1)
    qseg[...] = jnp.where(inside(low[0:1], high[0:1]) & (lanes < 3), 1.0, 0.0).astype(jnp.bfloat16)

    def send_own(part):
        @pl.when(chip < CHIPS - 1)
        def _():
            up_copy(0, part).start()

        for stream in range(2):

            @pl.when((core == stream) & (chip <= LAST[part]))
            def _():
                down_copy(0, part, stream).start()

        @pl.when(core == 0)
        def _():
            side_copy(chip, part).start()

    k_in.wait()
    pl.semaphore_wait(barrier, sum(partner.astype(jnp.int32) for partner in partners))
    send_own(0)
    v_in.wait()
    turned = vv[...].astype(jnp.float32).T.astype(jnp.bfloat16)
    for half in range(rows // HD):
        at = rows + SEG + half * HD
        kv[me, at : at + HD, :] = turned[:, half * HD : (half + 1) * HD]
    send_own(1)
    q_in.wait()

    def keys_of(block):
        bounds = kv[block, rows : rows + SEG, :].astype(jnp.float32)
        hidden = jnp.where(inside(bounds[0:1], bounds[8:9]), 0.0, HIDE).astype(jnp.bfloat16)
        return jnp.concatenate([kv[block, 0:rows, :], hidden], axis=1)

    def values_of(block):
        first = rows + SEG
        return [kv[block, first + i * HD : first + (i + 1) * HD, :] for i in range(rows // HD)]

    def scores(keys, h):
        query = jnp.concatenate([qv[:, h * HD : (h + 1) * HD], qseg[...]], axis=1)
        return [
            lax.dot_general(
                block, query, (((1,), (1,)), ((), ())), preferred_element_type=jnp.float32
            )
            for block in keys
        ]

    def attend(blocks, own=False):
        keys = [keys_of(block) for block in blocks]
        values = jnp.concatenate([piece for block in blocks for piece in values_of(block)], axis=1)
        ones = jnp.ones((ONES, values.shape[1]), jnp.bfloat16)
        values = jnp.concatenate([values, ones], axis=0)

        def finish(h, weight, alpha):
            part = jnp.dot(values, weight, preferred_element_type=jnp.float32)[: HD + 8]
            acc[h] = part if own else acc[h] * alpha + part

        ahead, behind = [scores(keys, h) for h in range(AHEAD)], None
        for h in range(heads):
            score = ahead.pop(0)
            if h + AHEAD < heads:
                ahead.append(scores(keys, h + AHEAD))
            if own:
                u = lax.broadcasted_iota(jnp.int32, (rows, rows), 0)
                t = lax.broadcasted_iota(jnp.int32, (rows, rows), 1)
                score = [jnp.where(u <= t, score[0], HIDE)]
            new, alpha = None, None
            for piece in score:
                most = jnp.max(piece, axis=0, keepdims=True)
                new = most if new is None else jnp.maximum(new, most)
            if not own:
                old = top[h : h + 1, :]
                new = jnp.maximum(old, new)
                alpha = jnp.exp2((old - new) * factor)
            weight = [jnp.exp2((piece - new) * factor).astype(jnp.bfloat16) for piece in score]
            top[h : h + 1, :] = new
            if behind is not None:
                finish(*behind)
            behind = (h, jnp.concatenate(weight, axis=0), alpha)
        finish(*behind)

    attend([me], own=True)

    def relay_up(hop, part):
        @pl.when(up_comes(hop, part))
        def _():
            arrived((chip - hop) * 2 + core, part)

            @pl.when(up_goes(hop, part))
            def _():
                up_copy(hop, part).start()

            side_copy(chip - hop, part).start()

    def relay_down(hop, part):
        source = lax.rem(chip + hop, CHIPS)

        def pass_on(stream):
            @pl.when(down_comes(hop, part, stream))
            def _():
                arrived(source * 2 + stream, part)

                @pl.when(down_goes(hop, part, stream))
                def _():
                    down_copy(hop, part, stream).start()

                @pl.when(down_hands(hop, part, stream))
                def _():
                    side_copy(source, part).start()

        pass_on(jnp.where(chip == 0, 0, core))

        @pl.when(chip == 0)
        def _():
            pass_on(1)

    def handed(block):
        for part in range(2):
            arrived(block, part)

    def one_round(hop, carry):
        below_source = jnp.where(chip == 0, 0, chip - hop)
        above_source = lax.rem(chip + hop, CHIPS)
        first = (chip == 1) | (chip == CHIPS - 1)
        early = (chip == CHIPS - 2) & (hop == 2)

        @pl.when(hop >= 1)
        def _():
            for part in range(2):
                done = (chip == CHIPS - 2) & (hop == 3) & (part == 0)

                @pl.when(first)
                def _():
                    relay_down(hop, part)

                @pl.when(jnp.logical_not(done))
                def _():
                    relay_up(hop, part)

                @pl.when(jnp.logical_not(first | done))
                def _():
                    relay_down(hop, part)

        pair = down_pair(hop)
        short = pair & (hop == 2) & (core == 1)
        doubles = jnp.where(short, 1, 2) * pair.astype(jnp.int32)
        alone = jnp.where(pair, 0, 2 * (chip >= hop).astype(jnp.int32))
        alone = jnp.where(short, 1, jnp.where(hop == 0, core, alone))
        alone = jnp.where(chip == 0, jnp.where(hop == 4, core, 0), alone)
        second = short | (hop == 0) | (chip == 0)

        def one_double(i, carry):
            @pl.when(i == 1)
            def _():
                handed(below_source * 2 + 1 - core)
                handed(above_source * 2 + 1 - core)

            side = jnp.where(i == 1, 1 - core, core)
            attend([below_source * 2 + side, above_source * 2 + side])

            @pl.when(early & (i == 0))
            def _():
                relay_up(hop + 1, 0)
                relay_down(hop + 1, 0)

            return carry

        def one_block(i, carry):
            other = (i == 1) | second

            @pl.when(other)
            def _():
                handed(below_source * 2 + 1 - core)

            attend([below_source * 2 + jnp.where(other, 1 - core, core)])
            return carry

        lax.fori_loop(0, doubles, one_double, 0)
        lax.fori_loop(0, alone, one_block, 0)
        return carry

    lax.fori_loop(0, 5, one_round, 0)

    for h in range(heads):
        share = acc[h, 0:HD, :] * (1.0 / acc[h, HD : HD + 1, :])
        out_ref[:, h * HD : (h + 1) * HD] = share.astype(jnp.bfloat16).T

    for part in range(2):

        @pl.when(core == 0)
        def _():
            side_copy(chip, part).wait_send()

        for hop in range(4):

            @pl.when(up_goes(hop, part))
            def _():
                up_copy(hop, part).wait_send()

            for stream in range(2):

                @pl.when(down_goes(hop, part, stream))
                def _():
                    down_copy(hop, part, stream).wait_send()

        for hop in range(1, 5):

            @pl.when(up_comes(hop, part))
            def _():
                side_copy(chip - hop, part).wait_send()

            for stream in range(2):

                @pl.when(down_hands(hop, part, stream))
                def _():
                    side_copy(lax.rem(chip + hop, CHIPS), part).wait_send()


def per_device(queries, keys, values, segment_ids):
    rows, width = queries.shape
    heads = width // HD
    size = 2 * rows + SEG
    operands = (queries, keys, values, segment_ids.reshape(rows // HD, HD))
    operands = [pltpu.with_memory_space_constraint(operand, pltpu.HBM) for operand in operands]
    return pl.pallas_call(
        kernel,
        out_shape=pltpu.VMEM((rows, width), jnp.bfloat16),
        in_specs=[pl.BlockSpec(memory_space=pltpu.HBM)] * 4,
        out_specs=pl.BlockSpec(memory_space=pltpu.VMEM),
        scratch_shapes=[
            pltpu.VMEM((2 * CHIPS, size, HD), jnp.bfloat16),
            pltpu.VMEM((rows, width), jnp.bfloat16),
            pltpu.VMEM((rows, HD), jnp.bfloat16),
            pltpu.VMEM((rows // HD, HD), jnp.int32),
            pltpu.VMEM((rows, HD), jnp.bfloat16),
            pltpu.VMEM((heads, rows), jnp.float32),
            pltpu.VMEM((heads, HD + 8, rows), jnp.float32),
            pltpu.SemaphoreType.DMA((4,)),
            pltpu.SemaphoreType.DMA((2 * CHIPS, 2)),
            pltpu.SemaphoreType.DMA((4, 2)),
            pltpu.SemaphoreType.DMA((4, 2, 2)),
            pltpu.SemaphoreType.DMA((CHIPS, 2)),
        ],
        compiler_params=pltpu.CompilerParams(
            collective_id=0, has_side_effects=True, vmem_limit_bytes=32 * 1024 * 1024
        ),
        cost_estimate=pl.CostEstimate(
            flops=4 * rows * rows * 13 * width,
            bytes_accessed=4 * rows * width,
            transcendentals=13 * rows * rows * heads,
        ),
        name="ring_attention",
    )(*operands)


def solution(mesh):
    in_specs = (
        P(("dp", "ctx"), "head"),
        P(("dp", "ctx"), "head"),
        P(("dp", "ctx"), "head"),
        P(("dp", "ctx")),
    )
    out_specs = P(("dp", "ctx"), "head")
    return jax.shard_map(
        per_device, mesh=mesh, in_specs=in_specs, out_specs=out_specs, check_vma=False
    )
```

```python
import functools
import math

import jax
import jax.numpy as jnp
from jax import lax
from jax.experimental import pallas as pl
from jax.experimental.pallas import tpu as pltpu
from jax.sharding import PartitionSpec as P

HD = 128
MESH = pl.DeviceIdType.MESH
CHIPS = 8
SEG = 16
ONES = 16
HIDE = -(2.0**30)
AHEAD = 2
UP = (4, 3)
DOWN = 4
LAST = (2, 3)


def kernel(
    q_ref, k_ref, v_ref, seg_ref, out_ref,
    kv, qv, vv, sv, qseg, top, acc,
    in_sem, recv_sem, up_sem, down_sem, side_sem,
):
    rows = k_ref.shape[0]
    heads = q_ref.shape[1] // HD
    factor = math.log2(math.e) * HD**-0.5
    me = lax.axis_index("ctx")
    chip, core = me // 2, me % 2
    sibling = chip * 2 + 1 - core
    above_chip, below_chip = lax.rem(chip + 1, CHIPS), lax.rem(chip + CHIPS - 1, CHIPS)

    def up_comes(hop, part):
        return (chip >= hop) & ((hop <= 3) | ((hop <= UP[part]) & (chip == CHIPS - 1)))

    def up_goes(hop, part):
        return (chip >= hop) & (chip < CHIPS - 1) & ((hop < 3) | ((hop < UP[part]) & (chip == CHIPS - 2)))

    def down_passes(stream):
        return jnp.where(chip == 0, core == 1, core == stream)

    def down_comes(hop, part, stream):
        here = (lax.rem(chip + hop, CHIPS) <= LAST[part]) & (hop >= 1) & (hop <= DOWN)
        return here & ((chip < CHIPS - 1) | (hop >= 2)) & down_passes(stream)

    def down_goes(hop, part, stream):
        own = (hop == 0) & (chip <= LAST[part]) & (core == stream)
        return own | (down_comes(hop, part, stream) & (hop < DOWN))

    def down_pair(hop):
        return (lax.rem(chip + hop, CHIPS) <= 2) & (chip >= 5) & (hop >= 2) & (hop <= 3)

    def down_hands(hop, part, stream):
        pair = down_pair(hop) & ((hop == 3) | (core == 1))
        return (pair | ((hop == 4) & (chip >= 4))) & down_comes(hop, part, stream)

    cuts = (pl.ds(0, rows), pl.ds(rows, SEG + rows))

    def remote(block, part, send, target):
        return pltpu.make_async_remote_copy(
            src_ref=kv.at[block, cuts[part]],
            dst_ref=kv.at[block, cuts[part]],
            send_sem=send,
            recv_sem=recv_sem.at[block, part],
            device_id={"ctx": target},
            device_id_type=MESH,
        )

    def up_copy(hop, part):
        return remote((chip - hop) * 2 + core, part, up_sem.at[hop, part], above_chip * 2 + core)

    def down_copy(hop, part, stream):
        block = lax.rem(chip + hop, CHIPS) * 2 + stream
        target = below_chip * 2 + jnp.where(chip == 1, 1, stream)
        target = jnp.where((chip == 0) & (hop == 0), (CHIPS - 2) * 2 + stream, target)
        return remote(block, part, down_sem.at[hop, part, stream], target)

    def side_copy(source, part):
        return remote(source * 2 + core, part, side_sem.at[source, part], sibling)

    def arrived(block, part):
        remote(block, part, side_sem.at[0, part], sibling).wait_recv()

    barrier = pltpu.get_barrier_semaphore()

    def greet(target):
        pl.semaphore_signal(barrier, inc=1, device_id={"ctx": target}, device_id_type=MESH)

    @pl.when(chip >= 1)
    def _():
        greet(below_chip * 2 + core)

    @pl.when((chip >= 1) & (chip != 3) & (chip < CHIPS - 1))
    def _():
        greet(above_chip * 2 + core)

    @pl.when(chip == CHIPS - 2)
    def _():
        greet(core)

    @pl.when(chip == CHIPS - 1)
    def _():
        greet(1)

    @pl.when((chip == 0) & (core == 1))
    def _():
        greet(2)
        greet(3)

    @pl.when((chip >= 1) | (core == 1))
    def _():
        greet(sibling)

    passer = (chip == 0) & (core == 1)
    partners = [chip < CHIPS - 1, chip != 4, passer, passer, (chip >= 1) | (core == 0)]

    k_in = pltpu.make_async_copy(k_ref, kv.at[me, pl.ds(0, rows)], in_sem.at[0])
    v_in = pltpu.make_async_copy(v_ref, vv, in_sem.at[1])
    q_in = pltpu.make_async_copy(q_ref, qv, in_sem.at[2])
    seg_in = pltpu.make_async_copy(seg_ref, sv, in_sem.at[3])
    k_in.start()
    seg_in.start()
    v_in.start()
    q_in.start()

    def send_own(part):
        @pl.when(chip < CHIPS - 1)
        def _():
            up_copy(0, part).start()

        @pl.when(chip <= LAST[part])
        def _():
            down_copy(0, part, core).start()

        @pl.when(core == 0)
        def _():
            side_copy(chip, part).start()

    k_in.wait()
    pl.semaphore_wait(barrier, sum(partner.astype(jnp.int32) for partner in partners))
    send_own(0)

    seg_in.wait()
    seg = sv[...]
    count = [
        jnp.sum(jnp.sum(jnp.where(seg <= d, 1.0, 0.0), axis=1, keepdims=True), axis=0, keepdims=True)
        for d in (0, 1)
    ]
    lane = lax.broadcasted_iota(jnp.int32, (8, HD), 1)
    low = jnp.where(lane == 1, count[0], jnp.where(lane == 2, count[1], 0.0))
    high = jnp.where(lane == 0, count[0], jnp.where(lane == 1, count[1], float(rows)))
    kv[me, rows : rows + SEG, :] = jnp.concatenate([low, high], axis=0).astype(jnp.bfloat16)
    v_in.wait()
    turned = vv[...].astype(jnp.float32).T.astype(jnp.bfloat16)
    for half in range(rows // HD):
        at = rows + SEG + half * HD
        kv[me, at : at + HD, :] = turned[:, half * HD : (half + 1) * HD]
    send_own(1)

    def inside(low, high):
        place = lax.broadcasted_iota(jnp.int32, (rows, HD), 0).astype(jnp.float32)
        return (place >= low) & (place < high)

    lanes = lax.broadcasted_iota(jnp.int32, (rows, HD), 1)
    qseg[...] = jnp.where(inside(low[0:1], high[0:1]) & (lanes < 3), 1.0, 0.0).astype(jnp.bfloat16)
    q_in.wait()

    def keys_of(block):
        bounds = kv[block, rows : rows + SEG, :].astype(jnp.float32)
        hidden = jnp.where(inside(bounds[0:1], bounds[8:9]), 0.0, HIDE).astype(jnp.bfloat16)
        return jnp.concatenate([kv[block, 0:rows, :], hidden], axis=1)

    def values_of(block):
        first = rows + SEG
        return [kv[block, first + i * HD : first + (i + 1) * HD, :] for i in range(rows // HD)]

    def scores(keys, h):
        query = jnp.concatenate([qv[:, h * HD : (h + 1) * HD], qseg[...]], axis=1)
        return [
            lax.dot_general(
                block, query, (((1,), (1,)), ((), ())), preferred_element_type=jnp.float32
            )
            for block in keys
        ]

    def attend(blocks, own=False):
        keys = [keys_of(block) for block in blocks]
        values = jnp.concatenate([piece for block in blocks for piece in values_of(block)], axis=1)
        ones = jnp.ones((ONES, values.shape[1]), jnp.bfloat16)
        values = jnp.concatenate([values, ones], axis=0)

        def finish(h, weight, alpha):
            part = jnp.dot(values, weight, preferred_element_type=jnp.float32)[: HD + 8]
            acc[h] = part if own else acc[h] * alpha + part

        ahead, behind = [scores(keys, h) for h in range(AHEAD)], None
        for h in range(heads):
            score = ahead.pop(0)
            if h + AHEAD < heads:
                ahead.append(scores(keys, h + AHEAD))
            if own:
                u = lax.broadcasted_iota(jnp.int32, (rows, rows), 0)
                t = lax.broadcasted_iota(jnp.int32, (rows, rows), 1)
                score = [jnp.where(u <= t, score[0], HIDE)]
            new, alpha = None, None
            for piece in score:
                most = jnp.max(piece, axis=0, keepdims=True)
                new = most if new is None else jnp.maximum(new, most)
            if not own:
                old = top[h : h + 1, :]
                new = jnp.maximum(old, new)
                alpha = jnp.exp2((old - new) * factor)
            weight = [jnp.exp2((piece - new) * factor).astype(jnp.bfloat16) for piece in score]
            top[h : h + 1, :] = new
            if behind is not None:
                finish(*behind)
            behind = (h, jnp.concatenate(weight, axis=0), alpha)
        finish(*behind)

    attend([me], own=True)

    def relay_up(hop, part):
        @pl.when(up_comes(hop, part))
        def _():
            arrived((chip - hop) * 2 + core, part)

            @pl.when(up_goes(hop, part))
            def _():
                up_copy(hop, part).start()

            side_copy(chip - hop, part).start()

    def relay_down(hop, part):
        source = lax.rem(chip + hop, CHIPS)

        def pass_on(stream):
            @pl.when(down_comes(hop, part, stream))
            def _():
                arrived(source * 2 + stream, part)

                @pl.when(down_goes(hop, part, stream))
                def _():
                    down_copy(hop, part, stream).start()

                @pl.when(down_hands(hop, part, stream))
                def _():
                    side_copy(source, part).start()

        pass_on(jnp.where(chip == 0, 0, core))

        @pl.when(chip == 0)
        def _():
            pass_on(1)

    def handed(block):
        for part in range(2):
            arrived(block, part)

    def one_round(hop, carry):
        below_source = jnp.where(chip == 0, 0, chip - hop)
        above_source = lax.rem(chip + hop, CHIPS)
        first = (chip == 1) | (chip == CHIPS - 1)

        @pl.when(hop >= 1)
        def _():
            for part in range(2):

                @pl.when(first)
                def _():
                    relay_down(hop, part)

                relay_up(hop, part)

                @pl.when(jnp.logical_not(first))
                def _():
                    relay_down(hop, part)

        pair = down_pair(hop)
        short = pair & (hop == 2) & (core == 1)
        doubles = jnp.where(short, 1, 2) * pair.astype(jnp.int32)
        alone = jnp.where(pair, 0, 2 * (chip >= hop).astype(jnp.int32))
        alone = jnp.where(short, 1, jnp.where(hop == 0, core, alone))
        alone = jnp.where(chip == 0, jnp.where(hop == 4, core, 0), alone)
        second = short | (hop == 0) | (chip == 0)

        def one_double(i, carry):
            @pl.when(i == 1)
            def _():
                handed(below_source * 2 + 1 - core)
                handed(above_source * 2 + 1 - core)

            side = jnp.where(i == 1, 1 - core, core)
            attend([below_source * 2 + side, above_source * 2 + side])
            return carry

        def one_block(i, carry):
            other = (i == 1) | second

            @pl.when(other)
            def _():
                handed(below_source * 2 + 1 - core)

            attend([below_source * 2 + jnp.where(other, 1 - core, core)])
            return carry

        lax.fori_loop(0, doubles, one_double, 0)
        lax.fori_loop(0, alone, one_block, 0)
        return carry

    lax.fori_loop(0, 5, one_round, 0)

    for h in range(heads):
        share = acc[h, 0:HD, :] * (1.0 / acc[h, HD : HD + 1, :])
        out_ref[:, h * HD : (h + 1) * HD] = share.astype(jnp.bfloat16).T

    for part in range(2):

        @pl.when(core == 0)
        def _():
            side_copy(chip, part).wait_send()

        def sent_up(hop, carry):
            up_copy(hop, part).wait_send()
            return carry

        def handed_over(hop, carry):
            side_copy(chip - hop, part).wait_send()
            return carry

        most = jnp.where(chip == CHIPS - 2, UP[part] - 1, 2)
        lax.fori_loop(0, jnp.where(chip == CHIPS - 1, 0, jnp.minimum(chip, most) + 1), sent_up, 0)
        most = jnp.where(chip == CHIPS - 1, UP[part], 3)
        lax.fori_loop(1, jnp.minimum(chip, most) + 1, handed_over, 0)

        for hop in range(4):
            stream = jnp.where((chip == 0) & (hop > 0), 0, core)

            @pl.when(down_goes(hop, part, stream))
            def _():
                down_copy(hop, part, stream).wait_send()

        @pl.when((chip == 0) & (core == 1))
        def _():
            for hop in range(1, 4):

                @pl.when(down_goes(hop, part, 1))
                def _():
                    down_copy(hop, part, 1).wait_send()

        @pl.when(chip >= 4)
        def _():
            for hop in range(2, 5):

                @pl.when(down_hands(hop, part, core))
                def _():
                    side_copy(lax.rem(chip + hop, CHIPS), part).wait_send()


def per_device(queries, keys, values, segment_ids):
    rows, width = queries.shape
    heads = width // HD
    size = 2 * rows + SEG
    operands = (queries, keys, values, segment_ids.reshape(rows // HD, HD))
    operands = [pltpu.with_memory_space_constraint(operand, pltpu.HBM) for operand in operands]
    return pl.pallas_call(
        kernel,
        out_shape=pltpu.VMEM((rows, width), jnp.bfloat16),
        in_specs=[pl.BlockSpec(memory_space=pltpu.HBM)] * 4,
        out_specs=pl.BlockSpec(memory_space=pltpu.VMEM),
        scratch_shapes=[
            pltpu.VMEM((2 * CHIPS, size, HD), jnp.bfloat16),
            pltpu.VMEM((rows, width), jnp.bfloat16),
            pltpu.VMEM((rows, HD), jnp.bfloat16),
            pltpu.VMEM((rows // HD, HD), jnp.int32),
            pltpu.VMEM((rows, HD), jnp.bfloat16),
            pltpu.VMEM((heads, rows), jnp.float32),
            pltpu.VMEM((heads, HD + 8, rows), jnp.float32),
            pltpu.SemaphoreType.DMA((4,)),
            pltpu.SemaphoreType.DMA((2 * CHIPS, 2)),
            pltpu.SemaphoreType.DMA((4, 2)),
            pltpu.SemaphoreType.DMA((4, 2, 2)),
            pltpu.SemaphoreType.DMA((CHIPS, 2)),
        ],
        compiler_params=pltpu.CompilerParams(
            collective_id=0, has_side_effects=True, vmem_limit_bytes=32 * 1024 * 1024
        ),
        cost_estimate=pl.CostEstimate(
            flops=4 * rows * rows * 13 * width,
            bytes_accessed=4 * rows * width,
            transcendentals=13 * rows * rows * heads,
        ),
        name="ring_attention",
    )(*operands)


def solution(mesh):
    in_specs = (
        P(("dp", "ctx"), "head"),
        P(("dp", "ctx"), "head"),
        P(("dp", "ctx"), "head"),
        P(("dp", "ctx")),
    )
    out_specs = P(("dp", "ctx"), "head")
    return jax.shard_map(
        per_device, mesh=mesh, in_specs=in_specs, out_specs=out_specs, check_vma=False
    )
```

```python
import functools
import math

import jax
import jax.numpy as jnp
from jax import lax
from jax.experimental import pallas as pl
from jax.experimental.pallas import tpu as pltpu
from jax.sharding import PartitionSpec as P

HD = 128
MESH = pl.DeviceIdType.MESH
CHIPS = 8
SEG = 16
ONES = 16
HIDE = -(2.0**30)
AHEAD = 2
UP = (4, 3)
DOWN = 4
LAST = (2, 3)


def kernel(
    q_ref, k_ref, v_ref, seg_ref, out_ref,
    kv, qv, vv, sv, qseg, top, acc,
    in_sem, recv_sem, up_sem, down_sem, side_sem,
):
    rows = k_ref.shape[0]
    heads = q_ref.shape[1] // HD
    factor = math.log2(math.e) * HD**-0.5
    me = lax.axis_index("ctx")
    chip, core = me // 2, me % 2
    sibling = chip * 2 + 1 - core
    above_chip, below_chip = lax.rem(chip + 1, CHIPS), lax.rem(chip + CHIPS - 1, CHIPS)

    def up_comes(hop, part):
        return (chip >= hop) & ((hop <= 3) | ((hop <= UP[part]) & (chip == CHIPS - 1)))

    def up_goes(hop, part):
        return (chip >= hop) & (chip < CHIPS - 1) & ((hop < 3) | ((hop < UP[part]) & (chip == CHIPS - 2)))

    def down_passes(stream):
        return jnp.where(chip == 0, core == 1, core == stream)

    def down_comes(hop, part, stream):
        here = (lax.rem(chip + hop, CHIPS) <= LAST[part]) & (hop >= 1) & (hop <= DOWN)
        return here & ((chip < CHIPS - 1) | (hop >= 2)) & down_passes(stream)

    def down_goes(hop, part, stream):
        own = (hop == 0) & (chip <= LAST[part]) & (core == stream)
        return own | (down_comes(hop, part, stream) & (hop < DOWN))

    def down_pair(hop):
        return (lax.rem(chip + hop, CHIPS) <= 2) & (chip >= 5) & (hop >= 2) & (hop <= 3)

    def down_hands(hop, part, stream):
        pair = down_pair(hop) & ((hop == 3) | (core == 1))
        return (pair | ((hop == 4) & (chip >= 4))) & down_comes(hop, part, stream)

    cuts = (pl.ds(0, rows), pl.ds(rows, SEG + rows))

    def remote(block, part, send, target):
        return pltpu.make_async_remote_copy(
            src_ref=kv.at[block, cuts[part]],
            dst_ref=kv.at[block, cuts[part]],
            send_sem=send,
            recv_sem=recv_sem.at[block, part],
            device_id={"ctx": target},
            device_id_type=MESH,
        )

    def up_copy(hop, part):
        return remote((chip - hop) * 2 + core, part, up_sem.at[hop, part], above_chip * 2 + core)

    def down_copy(hop, part, stream):
        block = lax.rem(chip + hop, CHIPS) * 2 + stream
        target = below_chip * 2 + jnp.where(chip == 1, 1, stream)
        target = jnp.where((chip == 0) & (hop == 0), (CHIPS - 2) * 2 + stream, target)
        return remote(block, part, down_sem.at[hop, part, stream], target)

    def side_copy(source, part):
        return remote(source * 2 + core, part, side_sem.at[source, part], sibling)

    def arrived(block, part):
        remote(block, part, side_sem.at[0, part], sibling).wait_recv()

    barrier = pltpu.get_barrier_semaphore()

    def greet(target):
        pl.semaphore_signal(barrier, inc=1, device_id={"ctx": target}, device_id_type=MESH)

    @pl.when(chip >= 1)
    def _():
        greet(below_chip * 2 + core)

    @pl.when((chip >= 1) & (chip != 3) & (chip < CHIPS - 1))
    def _():
        greet(above_chip * 2 + core)

    @pl.when(chip == CHIPS - 2)
    def _():
        greet(core)

    @pl.when(chip == CHIPS - 1)
    def _():
        greet(1)

    @pl.when((chip == 0) & (core == 1))
    def _():
        greet(2)
        greet(3)

    @pl.when((chip >= 1) | (core == 1))
    def _():
        greet(sibling)

    passer = (chip == 0) & (core == 1)
    partners = [chip < CHIPS - 1, chip != 4, passer, passer, (chip >= 1) | (core == 0)]

    k_in = pltpu.make_async_copy(k_ref, kv.at[me, pl.ds(0, rows)], in_sem.at[0])
    v_in = pltpu.make_async_copy(v_ref, vv, in_sem.at[1])
    q_in = pltpu.make_async_copy(q_ref, qv, in_sem.at[2])
    seg_in = pltpu.make_async_copy(seg_ref, sv, in_sem.at[3])
    k_in.start()
    seg_in.start()
    v_in.start()
    q_in.start()

    def send_own(part):
        @pl.when(chip <= 2)
        def _():
            down_copy(0, part, core).start()

        @pl.when(chip < CHIPS - 1)
        def _():
            up_copy(0, part).start()

        @pl.when((chip > 2) & (chip <= LAST[part]))
        def _():
            down_copy(0, part, core).start()

    k_in.wait()
    pl.semaphore_wait(barrier, sum(partner.astype(jnp.int32) for partner in partners))
    send_own(0)

    seg_in.wait()
    seg = sv[...]
    count = [
        jnp.sum(jnp.sum(jnp.where(seg <= d, 1.0, 0.0), axis=1, keepdims=True), axis=0, keepdims=True)
        for d in (0, 1)
    ]
    lane = lax.broadcasted_iota(jnp.int32, (8, HD), 1)
    low = jnp.where(lane == 1, count[0], jnp.where(lane == 2, count[1], 0.0))
    high = jnp.where(lane == 0, count[0], jnp.where(lane == 1, count[1], float(rows)))
    kv[me, rows : rows + SEG, :] = jnp.concatenate([low, high], axis=0).astype(jnp.bfloat16)
    v_in.wait()
    turned = vv[...].astype(jnp.float32).T.astype(jnp.bfloat16)
    for half in range(rows // HD):
        at = rows + SEG + half * HD
        kv[me, at : at + HD, :] = turned[:, half * HD : (half + 1) * HD]
    send_own(1)

    @pl.when(core == 0)
    def _():
        for part in range(2):
            side_copy(chip, part).start()

    def inside(low, high):
        place = lax.broadcasted_iota(jnp.int32, (rows, HD), 0).astype(jnp.float32)
        return (place >= low) & (place < high)

    lanes = lax.broadcasted_iota(jnp.int32, (rows, HD), 1)
    qseg[...] = jnp.where(inside(low[0:1], high[0:1]) & (lanes < 3), 1.0, 0.0).astype(jnp.bfloat16)
    q_in.wait()

    def keys_of(block):
        bounds = kv[block, rows : rows + SEG, :].astype(jnp.float32)
        hidden = jnp.where(inside(bounds[0:1], bounds[8:9]), 0.0, HIDE).astype(jnp.bfloat16)
        return jnp.concatenate([kv[block, 0:rows, :], hidden], axis=1)

    def values_of(block):
        first = rows + SEG
        return [kv[block, first + i * HD : first + (i + 1) * HD, :] for i in range(rows // HD)]

    def scores(keys, h):
        query = jnp.concatenate([qv[:, h * HD : (h + 1) * HD], qseg[...]], axis=1)
        return [
            lax.dot_general(
                block, query, (((1,), (1,)), ((), ())), preferred_element_type=jnp.float32
            )
            for block in keys
        ]

    def attend(blocks, own=False):
        keys = [keys_of(block) for block in blocks]
        values = jnp.concatenate([piece for block in blocks for piece in values_of(block)], axis=1)
        ones = jnp.ones((ONES, values.shape[1]), jnp.bfloat16)
        values = jnp.concatenate([values, ones], axis=0)

        def finish(h, weight, alpha):
            part = jnp.dot(values, weight, preferred_element_type=jnp.float32)[: HD + 8]
            acc[h] = part if own else acc[h] * alpha + part

        ahead, behind = [scores(keys, h) for h in range(AHEAD)], None
        for h in range(heads):
            score = ahead.pop(0)
            if h + AHEAD < heads:
                ahead.append(scores(keys, h + AHEAD))
            if own:
                u = lax.broadcasted_iota(jnp.int32, (rows, rows), 0)
                t = lax.broadcasted_iota(jnp.int32, (rows, rows), 1)
                score = [jnp.where(u <= t, score[0], HIDE)]
            new, alpha = None, None
            for piece in score:
                most = jnp.max(piece, axis=0, keepdims=True)
                new = most if new is None else jnp.maximum(new, most)
            if not own:
                old = top[h : h + 1, :]
                new = jnp.maximum(old, new)
                alpha = jnp.exp2((old - new) * factor)
            weight = [jnp.exp2((piece - new) * factor).astype(jnp.bfloat16) for piece in score]
            top[h : h + 1, :] = new
            if behind is not None:
                finish(*behind)
            behind = (h, jnp.concatenate(weight, axis=0), alpha)
        finish(*behind)

    attend([me], own=True)

    def relay_up(hop, part):
        @pl.when(up_comes(hop, part))
        def _():
            arrived((chip - hop) * 2 + core, part)

            @pl.when(up_goes(hop, part))
            def _():
                up_copy(hop, part).start()

            side_copy(chip - hop, part).start()

    def relay_down(hop, part):
        source = lax.rem(chip + hop, CHIPS)

        def pass_on(stream):
            @pl.when(down_comes(hop, part, stream))
            def _():
                arrived(source * 2 + stream, part)

                @pl.when(down_goes(hop, part, stream))
                def _():
                    down_copy(hop, part, stream).start()

                @pl.when(down_hands(hop, part, stream))
                def _():
                    side_copy(source, part).start()

        pass_on(jnp.where(chip == 0, 0, core))

        @pl.when(chip == 0)
        def _():
            pass_on(1)

    def handed(block):
        for part in range(2):
            arrived(block, part)

    def one_round(hop, carry):
        below_source = jnp.where(chip == 0, 0, chip - hop)
        above_source = lax.rem(chip + hop, CHIPS)
        first = (chip == 1) | (chip == CHIPS - 1)

        @pl.when(hop >= 1)
        def _():
            for part in range(2):

                @pl.when(first)
                def _():
                    relay_down(hop, part)

                relay_up(hop, part)

                @pl.when(jnp.logical_not(first))
                def _():
                    relay_down(hop, part)

        pair = down_pair(hop)
        short = pair & (hop == 2) & (core == 1)
        doubles = jnp.where(short, 1, 2) * pair.astype(jnp.int32)
        alone = jnp.where(pair, 0, 2 * (chip >= hop).astype(jnp.int32))
        alone = jnp.where(short, 1, jnp.where(hop == 0, core, alone))
        alone = jnp.where(chip == 0, jnp.where(hop == 4, core, 0), alone)
        second = short | (hop == 0) | (chip == 0)

        def one_double(i, carry):
            @pl.when(i == 1)
            def _():
                handed(below_source * 2 + 1 - core)
                handed(above_source * 2 + 1 - core)

            side = jnp.where(i == 1, 1 - core, core)
            attend([below_source * 2 + side, above_source * 2 + side])
            return carry

        def one_block(i, carry):
            other = (i == 1) | second

            @pl.when(other)
            def _():
                handed(below_source * 2 + 1 - core)

            attend([below_source * 2 + jnp.where(other, 1 - core, core)])
            return carry

        lax.fori_loop(0, doubles, one_double, 0)
        lax.fori_loop(0, alone, one_block, 0)
        return carry

    lax.fori_loop(0, 5, one_round, 0)

    for h in range(heads):
        share = acc[h, 0:HD, :] * (1.0 / acc[h, HD : HD + 1, :])
        out_ref[:, h * HD : (h + 1) * HD] = share.astype(jnp.bfloat16).T

    for part in range(2):

        @pl.when(core == 0)
        def _():
            side_copy(chip, part).wait_send()

        def sent_up(hop, carry):
            up_copy(hop, part).wait_send()
            return carry

        def handed_over(hop, carry):
            side_copy(chip - hop, part).wait_send()
            return carry

        most = jnp.where(chip == CHIPS - 2, UP[part] - 1, 2)
        lax.fori_loop(0, jnp.where(chip == CHIPS - 1, 0, jnp.minimum(chip, most) + 1), sent_up, 0)
        most = jnp.where(chip == CHIPS - 1, UP[part], 3)
        lax.fori_loop(1, jnp.minimum(chip, most) + 1, handed_over, 0)

        for hop in range(4):
            stream = jnp.where((chip == 0) & (hop > 0), 0, core)

            @pl.when(down_goes(hop, part, stream))
            def _():
                down_copy(hop, part, stream).wait_send()

        @pl.when((chip == 0) & (core == 1))
        def _():
            for hop in range(1, 4):

                @pl.when(down_goes(hop, part, 1))
                def _():
                    down_copy(hop, part, 1).wait_send()

        @pl.when(chip >= 4)
        def _():
            for hop in range(2, 5):

                @pl.when(down_hands(hop, part, core))
                def _():
                    side_copy(lax.rem(chip + hop, CHIPS), part).wait_send()


def per_device(queries, keys, values, segment_ids):
    rows, width = queries.shape
    heads = width // HD
    size = 2 * rows + SEG
    operands = (queries, keys, values, segment_ids.reshape(rows // HD, HD))
    operands = [pltpu.with_memory_space_constraint(operand, pltpu.HBM) for operand in operands]
    return pl.pallas_call(
        kernel,
        out_shape=pltpu.VMEM((rows, width), jnp.bfloat16),
        in_specs=[pl.BlockSpec(memory_space=pltpu.HBM)] * 4,
        out_specs=pl.BlockSpec(memory_space=pltpu.VMEM),
        scratch_shapes=[
            pltpu.VMEM((2 * CHIPS, size, HD), jnp.bfloat16),
            pltpu.VMEM((rows, width), jnp.bfloat16),
            pltpu.VMEM((rows, HD), jnp.bfloat16),
            pltpu.VMEM((rows // HD, HD), jnp.int32),
            pltpu.VMEM((rows, HD), jnp.bfloat16),
            pltpu.VMEM((heads, rows), jnp.float32),
            pltpu.VMEM((heads, HD + 8, rows), jnp.float32),
            pltpu.SemaphoreType.DMA((4,)),
            pltpu.SemaphoreType.DMA((2 * CHIPS, 2)),
            pltpu.SemaphoreType.DMA((4, 2)),
            pltpu.SemaphoreType.DMA((4, 2, 2)),
            pltpu.SemaphoreType.DMA((CHIPS, 2)),
        ],
        compiler_params=pltpu.CompilerParams(
            collective_id=0, has_side_effects=True, vmem_limit_bytes=32 * 1024 * 1024
        ),
        cost_estimate=pl.CostEstimate(
            flops=4 * rows * rows * 13 * width,
            bytes_accessed=4 * rows * width,
            transcendentals=13 * rows * rows * heads,
        ),
        name="ring_attention",
    )(*operands)


def solution(mesh):
    in_specs = (
        P(("dp", "ctx"), "head"),
        P(("dp", "ctx"), "head"),
        P(("dp", "ctx"), "head"),
        P(("dp", "ctx")),
    )
    out_specs = P(("dp", "ctx"), "head")
    return jax.shard_map(
        per_device, mesh=mesh, in_specs=in_specs, out_specs=out_specs, check_vma=False
    )
```

```python
import functools
import math

import jax
import jax.numpy as jnp
from jax import lax
from jax.experimental import pallas as pl
from jax.experimental.pallas import tpu as pltpu
from jax.sharding import PartitionSpec as P

HD = 128
MESH = pl.DeviceIdType.MESH
CHIPS = 8
SEG = 16
ONES = 16
HIDE = -(2.0**30)
AHEAD = 2
UP = (4, 3)
DOWN = 4
LAST = (2, 3)


def kernel(
    q_ref, k_ref, v_ref, seg_ref, out_ref,
    kv, qv, vv, sv, qseg, top, acc,
    in_sem, recv_sem, up_sem, down_sem, side_sem,
):
    rows = k_ref.shape[0]
    heads = q_ref.shape[1] // HD
    factor = math.log2(math.e) * HD**-0.5
    me = lax.axis_index("ctx")
    chip, core = me // 2, me % 2
    sibling = chip * 2 + 1 - core
    above_chip, below_chip = lax.rem(chip + 1, CHIPS), lax.rem(chip + CHIPS - 1, CHIPS)

    def up_comes(hop, part):
        return (chip >= hop) & ((hop <= 3) | ((hop <= UP[part]) & (chip == CHIPS - 1)))

    def up_goes(hop, part):
        return (chip >= hop) & (chip < CHIPS - 1) & ((hop < 3) | ((hop < UP[part]) & (chip == CHIPS - 2)))

    def down_passes(stream):
        return jnp.where(chip == 0, core == 1, core == stream)

    def down_comes(hop, part, stream):
        here = (lax.rem(chip + hop, CHIPS) <= LAST[part]) & (hop >= 1) & (hop <= DOWN)
        return here & ((chip < CHIPS - 1) | (hop >= 2)) & down_passes(stream)

    def down_goes(hop, part, stream):
        own = (hop == 0) & (chip <= LAST[part]) & (core == stream)
        return own | (down_comes(hop, part, stream) & (hop < DOWN))

    def down_pair(hop):
        return (lax.rem(chip + hop, CHIPS) <= 2) & (chip >= 5) & (hop >= 2) & (hop <= 3)

    def down_hands(hop, part, stream):
        pair = down_pair(hop) & ((hop == 3) | (core == 1))
        return (pair | ((hop == 4) & (chip >= 4))) & down_comes(hop, part, stream)

    cuts = (pl.ds(0, rows), pl.ds(rows, SEG + rows))

    def remote(block, part, send, target):
        return pltpu.make_async_remote_copy(
            src_ref=kv.at[block, cuts[part]],
            dst_ref=kv.at[block, cuts[part]],
            send_sem=send,
            recv_sem=recv_sem.at[block, part],
            device_id={"ctx": target},
            device_id_type=MESH,
        )

    def up_copy(hop, part):
        return remote((chip - hop) * 2 + core, part, up_sem.at[hop, part], above_chip * 2 + core)

    def down_copy(hop, part, stream):
        block = lax.rem(chip + hop, CHIPS) * 2 + stream
        target = below_chip * 2 + jnp.where(chip == 1, 1, stream)
        target = jnp.where((chip == 0) & (hop == 0), (CHIPS - 2) * 2 + stream, target)
        return remote(block, part, down_sem.at[hop, part, stream], target)

    def side_copy(source, part):
        return remote(source * 2 + core, part, side_sem.at[source, part], sibling)

    def arrived(block, part):
        remote(block, part, side_sem.at[0, part], sibling).wait_recv()

    barrier = pltpu.get_barrier_semaphore()

    def greet(target):
        pl.semaphore_signal(barrier, inc=1, device_id={"ctx": target}, device_id_type=MESH)

    @pl.when(chip >= 1)
    def _():
        greet(below_chip * 2 + core)

    @pl.when((chip >= 1) & (chip != 3) & (chip < CHIPS - 1))
    def _():
        greet(above_chip * 2 + core)

    @pl.when(chip == CHIPS - 2)
    def _():
        greet(core)

    @pl.when(chip == CHIPS - 1)
    def _():
        greet(1)

    @pl.when((chip == 0) & (core == 1))
    def _():
        greet(2)
        greet(3)

    @pl.when((chip >= 1) | (core == 1))
    def _():
        greet(sibling)

    passer = (chip == 0) & (core == 1)
    partners = [chip < CHIPS - 1, chip != 4, passer, passer, (chip >= 1) | (core == 0)]

    k_in = pltpu.make_async_copy(k_ref, kv.at[me, pl.ds(0, rows)], in_sem.at[0])
    v_in = pltpu.make_async_copy(v_ref, vv, in_sem.at[1])
    q_in = pltpu.make_async_copy(q_ref, qv, in_sem.at[2])
    seg_in = pltpu.make_async_copy(seg_ref, sv, in_sem.at[3])
    k_in.start()
    seg_in.start()
    v_in.start()
    q_in.start()

    def send_own(part):
        @pl.when(chip <= 2)
        def _():
            down_copy(0, part, core).start()

        @pl.when(chip < CHIPS - 1)
        def _():
            up_copy(0, part).start()

        @pl.when((chip > 2) & (chip <= LAST[part]))
        def _():
            down_copy(0, part, core).start()

    k_in.wait()
    pl.semaphore_wait(barrier, sum(partner.astype(jnp.int32) for partner in partners))
    send_own(0)

    seg_in.wait()
    seg = sv[...]
    count = [
        jnp.sum(jnp.sum(jnp.where(seg <= d, 1.0, 0.0), axis=1, keepdims=True), axis=0, keepdims=True)
        for d in (0, 1)
    ]
    lane = lax.broadcasted_iota(jnp.int32, (8, HD), 1)
    low = jnp.where(lane == 1, count[0], jnp.where(lane == 2, count[1], 0.0))
    high = jnp.where(lane == 0, count[0], jnp.where(lane == 1, count[1], float(rows)))
    kv[me, rows : rows + SEG, :] = jnp.concatenate([low, high], axis=0).astype(jnp.bfloat16)
    v_in.wait()
    turned = vv[...].astype(jnp.float32).T.astype(jnp.bfloat16)
    for half in range(rows // HD):
        at = rows + SEG + half * HD
        kv[me, at : at + HD, :] = turned[:, half * HD : (half + 1) * HD]
    send_own(1)

    @pl.when(core == 0)
    def _():
        for part in range(2):
            side_copy(chip, part).start()

    def inside(low, high):
        place = lax.broadcasted_iota(jnp.int32, (rows, HD), 0).astype(jnp.float32)
        return (place >= low) & (place < high)

    lanes = lax.broadcasted_iota(jnp.int32, (rows, HD), 1)
    qseg[...] = jnp.where(inside(low[0:1], high[0:1]) & (lanes < 3), 1.0, 0.0).astype(jnp.bfloat16)
    q_in.wait()

    def keys_of(block):
        bounds = kv[block, rows : rows + SEG, :].astype(jnp.float32)
        hidden = jnp.where(inside(bounds[0:1], bounds[8:9]), 0.0, HIDE).astype(jnp.bfloat16)
        return jnp.concatenate([kv[block, 0:rows, :], hidden], axis=1)

    def values_of(block):
        first = rows + SEG
        return [kv[block, first + i * HD : first + (i + 1) * HD, :] for i in range(rows // HD)]

    def scores(keys, h):
        query = jnp.concatenate([qv[:, h * HD : (h + 1) * HD], qseg[...]], axis=1)
        return [
            lax.dot_general(
                block, query, (((1,), (1,)), ((), ())), preferred_element_type=jnp.float32
            )
            for block in keys
        ]

    def attend(blocks, own=False):
        keys = [keys_of(block) for block in blocks]
        values = jnp.concatenate([piece for block in blocks for piece in values_of(block)], axis=1)
        ones = jnp.ones((ONES, values.shape[1]), jnp.bfloat16)
        values = jnp.concatenate([values, ones], axis=0)

        def finish(h, weight, alpha):
            part = jnp.dot(values, weight, preferred_element_type=jnp.float32)[: HD + 8]
            acc[h] = part if own else acc[h] * alpha + part

        ahead, behind = [scores(keys, h) for h in range(AHEAD)], None
        for h in range(heads):
            score = ahead.pop(0)
            if h + AHEAD < heads:
                ahead.append(scores(keys, h + AHEAD))
            if own:
                u = lax.broadcasted_iota(jnp.int32, (rows, rows), 0)
                t = lax.broadcasted_iota(jnp.int32, (rows, rows), 1)
                score = [jnp.where(u <= t, score[0], HIDE)]
            new, alpha = None, None
            for piece in score:
                most = jnp.max(piece, axis=0, keepdims=True)
                new = most if new is None else jnp.maximum(new, most)
            if not own:
                old = top[h : h + 1, :]
                new = jnp.maximum(old, new)
                alpha = jnp.exp2((old - new) * factor)
            weight = [jnp.exp2((piece - new) * factor).astype(jnp.bfloat16) for piece in score]
            top[h : h + 1, :] = new
            if behind is not None:
                finish(*behind)
            behind = (h, jnp.concatenate(weight, axis=0), alpha)
        finish(*behind)

    attend([me], own=True)

    def relay_up(hop, part):
        @pl.when(up_comes(hop, part))
        def _():
            arrived((chip - hop) * 2 + core, part)

            @pl.when(up_goes(hop, part))
            def _():
                up_copy(hop, part).start()

            side_copy(chip - hop, part).start()

    def relay_down(hop, part):
        source = lax.rem(chip + hop, CHIPS)

        def pass_on(stream):
            @pl.when(down_comes(hop, part, stream))
            def _():
                arrived(source * 2 + stream, part)

                @pl.when(down_goes(hop, part, stream))
                def _():
                    down_copy(hop, part, stream).start()

                @pl.when(down_hands(hop, part, stream))
                def _():
                    side_copy(source, part).start()

        pass_on(jnp.where(chip == 0, 0, core))

        @pl.when(chip == 0)
        def _():
            pass_on(1)

    def handed(block):
        for part in range(2):
            arrived(block, part)

    def one_round(hop, carry):
        below_source = jnp.where(chip == 0, 0, chip - hop)
        above_source = lax.rem(chip + hop, CHIPS)
        first = (chip == 1) | (chip == CHIPS - 1)

        @pl.when(hop >= 1)
        def _():
            for part in range(2):

                @pl.when(first)
                def _():
                    relay_down(hop, part)

                relay_up(hop, part)

                @pl.when((chip == 0) | (chip == 2))
                def _():
                    relay_down(hop, part)

            @pl.when((chip >= 4) & (chip < CHIPS - 1))
            def _():
                for part in range(2):
                    relay_down(hop, part)

        pair = down_pair(hop)
        short = pair & (hop == 2) & (core == 1)
        doubles = jnp.where(short, 1, 2) * pair.astype(jnp.int32)
        alone = jnp.where(pair, 0, 2 * (chip >= hop).astype(jnp.int32))
        alone = jnp.where(short, 1, jnp.where(hop == 0, core, alone))
        alone = jnp.where(chip == 0, jnp.where(hop == 4, core, 0), alone)
        second = short | (hop == 0) | (chip == 0)

        def one_double(i, carry):
            @pl.when(i == 1)
            def _():
                handed(below_source * 2 + 1 - core)
                handed(above_source * 2 + 1 - core)

            side = jnp.where(i == 1, 1 - core, core)
            attend([below_source * 2 + side, above_source * 2 + side])
            return carry

        def one_block(i, carry):
            other = (i == 1) | second

            @pl.when(other)
            def _():
                handed(below_source * 2 + 1 - core)

            attend([below_source * 2 + jnp.where(other, 1 - core, core)])
            return carry

        lax.fori_loop(0, doubles, one_double, 0)
        lax.fori_loop(0, alone, one_block, 0)
        return carry

    lax.fori_loop(0, 5, one_round, 0)

    for h in range(heads):
        share = acc[h, 0:HD, :] * (1.0 / acc[h, HD : HD + 1, :])
        out_ref[:, h * HD : (h + 1) * HD] = share.astype(jnp.bfloat16).T

    for part in range(2):

        @pl.when(core == 0)
        def _():
            side_copy(chip, part).wait_send()

        def sent_up(hop, carry):
            up_copy(hop, part).wait_send()
            return carry

        def handed_over(hop, carry):
            side_copy(chip - hop, part).wait_send()
            return carry

        most = jnp.where(chip == CHIPS - 2, UP[part] - 1, 2)
        lax.fori_loop(0, jnp.where(chip == CHIPS - 1, 0, jnp.minimum(chip, most) + 1), sent_up, 0)
        most = jnp.where(chip == CHIPS - 1, UP[part], 3)
        lax.fori_loop(1, jnp.minimum(chip, most) + 1, handed_over, 0)

        for hop in range(4):
            stream = jnp.where((chip == 0) & (hop > 0), 0, core)

            @pl.when(down_goes(hop, part, stream))
            def _():
                down_copy(hop, part, stream).wait_send()

        @pl.when((chip == 0) & (core == 1))
        def _():
            for hop in range(1, 4):

                @pl.when(down_goes(hop, part, 1))
                def _():
                    down_copy(hop, part, 1).wait_send()

        @pl.when(chip >= 4)
        def _():
            for hop in range(2, 5):

                @pl.when(down_hands(hop, part, core))
                def _():
                    side_copy(lax.rem(chip + hop, CHIPS), part).wait_send()


def per_device(queries, keys, values, segment_ids):
    rows, width = queries.shape
    heads = width // HD
    size = 2 * rows + SEG
    operands = (queries, keys, values, segment_ids.reshape(rows // HD, HD))
    operands = [pltpu.with_memory_space_constraint(operand, pltpu.HBM) for operand in operands]
    return pl.pallas_call(
        kernel,
        out_shape=pltpu.VMEM((rows, width), jnp.bfloat16),
        in_specs=[pl.BlockSpec(memory_space=pltpu.HBM)] * 4,
        out_specs=pl.BlockSpec(memory_space=pltpu.VMEM),
        scratch_shapes=[
            pltpu.VMEM((2 * CHIPS, size, HD), jnp.bfloat16),
            pltpu.VMEM((rows, width), jnp.bfloat16),
            pltpu.VMEM((rows, HD), jnp.bfloat16),
            pltpu.VMEM((rows // HD, HD), jnp.int32),
            pltpu.VMEM((rows, HD), jnp.bfloat16),
            pltpu.VMEM((heads, rows), jnp.float32),
            pltpu.VMEM((heads, HD + 8, rows), jnp.float32),
            pltpu.SemaphoreType.DMA((4,)),
            pltpu.SemaphoreType.DMA((2 * CHIPS, 2)),
            pltpu.SemaphoreType.DMA((4, 2)),
            pltpu.SemaphoreType.DMA((4, 2, 2)),
            pltpu.SemaphoreType.DMA((CHIPS, 2)),
        ],
        compiler_params=pltpu.CompilerParams(
            collective_id=0, has_side_effects=True, vmem_limit_bytes=32 * 1024 * 1024
        ),
        cost_estimate=pl.CostEstimate(
            flops=4 * rows * rows * 13 * width,
            bytes_accessed=4 * rows * width,
            transcendentals=13 * rows * rows * heads,
        ),
        name="ring_attention",
    )(*operands)


def solution(mesh):
    in_specs = (
        P(("dp", "ctx"), "head"),
        P(("dp", "ctx"), "head"),
        P(("dp", "ctx"), "head"),
        P(("dp", "ctx")),
    )
    out_specs = P(("dp", "ctx"), "head")
    return jax.shard_map(
        per_device, mesh=mesh, in_specs=in_specs, out_specs=out_specs, check_vma=False
    )
```

```python
import functools
import math

import jax
import jax.numpy as jnp
from jax import lax
from jax.experimental import pallas as pl
from jax.experimental.pallas import tpu as pltpu
from jax.sharding import PartitionSpec as P

HD = 128
MESH = pl.DeviceIdType.MESH
CHIPS = 8
SEG = 16
ONES = 16
HIDE = -(2.0**30)
AHEAD = 2
UP = (4, 3)
DOWN = 4
LAST = (2, 3)


def kernel(
    q_ref, k_ref, v_ref, seg_ref, out_ref,
    kv, qv, vv, sv, qseg, top, acc,
    in_sem, recv_sem, up_sem, down_sem, side_sem,
):
    rows = k_ref.shape[0]
    heads = q_ref.shape[1] // HD
    factor = math.log2(math.e) * HD**-0.5
    me = lax.axis_index("ctx")
    chip, core = me // 2, me % 2
    sibling = chip * 2 + 1 - core
    above_chip, below_chip = lax.rem(chip + 1, CHIPS), lax.rem(chip + CHIPS - 1, CHIPS)

    def up_comes(hop, part):
        return (chip >= hop) & ((hop <= 3) | ((hop <= UP[part]) & (chip == CHIPS - 1)))

    def up_goes(hop, part):
        return (chip >= hop) & (chip < CHIPS - 1) & ((hop < 3) | ((hop < UP[part]) & (chip == CHIPS - 2)))

    def down_passes(stream):
        return jnp.where(chip == 0, core == 1, core == stream)

    def down_comes(hop, part, stream):
        here = (lax.rem(chip + hop, CHIPS) <= LAST[part]) & (hop >= 1) & (hop <= DOWN)
        return here & ((chip < CHIPS - 1) | (hop >= 2)) & down_passes(stream)

    def down_goes(hop, part, stream):
        own = (hop == 0) & (chip <= LAST[part]) & (core == stream)
        return own | (down_comes(hop, part, stream) & (hop < DOWN))

    def down_pair(hop):
        return (lax.rem(chip + hop, CHIPS) <= 2) & (chip >= 5) & (hop >= 2) & (hop <= 3)

    def down_hands(hop, part, stream):
        pair = down_pair(hop) & ((hop == 3) | (core == 1))
        return (pair | ((hop == 4) & (chip >= 4))) & down_comes(hop, part, stream)

    cuts = (pl.ds(0, rows), pl.ds(rows, SEG + rows))

    def remote(block, part, send, target):
        return pltpu.make_async_remote_copy(
            src_ref=kv.at[block, cuts[part]],
            dst_ref=kv.at[block, cuts[part]],
            send_sem=send,
            recv_sem=recv_sem.at[block, part],
            device_id={"ctx": target},
            device_id_type=MESH,
        )

    def up_copy(hop, part):
        return remote((chip - hop) * 2 + core, part, up_sem.at[hop, part], above_chip * 2 + core)

    def down_copy(hop, part, stream):
        block = lax.rem(chip + hop, CHIPS) * 2 + stream
        target = below_chip * 2 + jnp.where(chip == 1, 1, stream)
        target = jnp.where((chip == 0) & (hop == 0), (CHIPS - 2) * 2 + stream, target)
        return remote(block, part, down_sem.at[hop, part, stream], target)

    def side_copy(source, part):
        return remote(source * 2 + core, part, side_sem.at[source, part], sibling)

    def arrived(block, part):
        remote(block, part, side_sem.at[0, part], sibling).wait_recv()

    barrier = pltpu.get_barrier_semaphore()

    def greet(target):
        pl.semaphore_signal(barrier, inc=1, device_id={"ctx": target}, device_id_type=MESH)

    @pl.when(chip >= 1)
    def _():
        greet(below_chip * 2 + core)

    @pl.when((chip >= 1) & (chip != 3) & (chip < CHIPS - 1))
    def _():
        greet(above_chip * 2 + core)

    @pl.when(chip == CHIPS - 2)
    def _():
        greet(core)

    @pl.when(chip == CHIPS - 1)
    def _():
        greet(1)

    @pl.when((chip == 0) & (core == 1))
    def _():
        greet(2)
        greet(3)

    @pl.when((chip >= 1) | (core == 1))
    def _():
        greet(sibling)

    passer = (chip == 0) & (core == 1)
    partners = [chip < CHIPS - 1, chip != 4, passer, passer, (chip >= 1) | (core == 0)]

    k_in = pltpu.make_async_copy(k_ref, kv.at[me, pl.ds(0, rows)], in_sem.at[0])
    v_in = pltpu.make_async_copy(v_ref, vv, in_sem.at[1])
    q_in = pltpu.make_async_copy(q_ref, qv, in_sem.at[2])
    seg_in = pltpu.make_async_copy(seg_ref, sv, in_sem.at[3])
    k_in.start()
    seg_in.start()
    v_in.start()
    q_in.start()

    def send_own(part):
        @pl.when(chip <= 2)
        def _():
            down_copy(0, part, core).start()

        @pl.when(chip < CHIPS - 1)
        def _():
            up_copy(0, part).start()

        @pl.when((chip > 2) & (chip <= LAST[part]))
        def _():
            down_copy(0, part, core).start()

    k_in.wait()
    pl.semaphore_wait(barrier, sum(partner.astype(jnp.int32) for partner in partners))
    send_own(0)

    seg_in.wait()
    seg = sv[...]
    count = [
        jnp.sum(jnp.sum(jnp.where(seg <= d, 1.0, 0.0), axis=1, keepdims=True), axis=0, keepdims=True)
        for d in (0, 1)
    ]
    lane = lax.broadcasted_iota(jnp.int32, (8, HD), 1)
    low = jnp.where(lane == 1, count[0], jnp.where(lane == 2, count[1], 0.0))
    high = jnp.where(lane == 0, count[0], jnp.where(lane == 1, count[1], float(rows)))
    kv[me, rows : rows + SEG, :] = jnp.concatenate([low, high], axis=0).astype(jnp.bfloat16)
    v_in.wait()
    turned = vv[...].astype(jnp.float32).T.astype(jnp.bfloat16)
    for half in range(rows // HD):
        at = rows + SEG + half * HD
        kv[me, at : at + HD, :] = turned[:, half * HD : (half + 1) * HD]
    send_own(1)

    @pl.when(core == 0)
    def _():
        for part in range(2):
            side_copy(chip, part).start()

    def inside(low, high):
        place = lax.broadcasted_iota(jnp.int32, (rows, HD), 0).astype(jnp.float32)
        return (place >= low) & (place < high)

    lanes = lax.broadcasted_iota(jnp.int32, (rows, HD), 1)
    qseg[...] = jnp.where(inside(low[0:1], high[0:1]) & (lanes < 3), 1.0, 0.0).astype(jnp.bfloat16)
    q_in.wait()

    def keys_of(block):
        bounds = kv[block, rows : rows + SEG, :].astype(jnp.float32)
        hidden = jnp.where(inside(bounds[0:1], bounds[8:9]), 0.0, HIDE).astype(jnp.bfloat16)
        return jnp.concatenate([kv[block, 0:rows, :], hidden], axis=1)

    def values_of(block):
        first = rows + SEG
        return [kv[block, first + i * HD : first + (i + 1) * HD, :] for i in range(rows // HD)]

    def scores(keys, h):
        query = jnp.concatenate([qv[:, h * HD : (h + 1) * HD], qseg[...]], axis=1)
        return [
            lax.dot_general(
                block, query, (((1,), (1,)), ((), ())), preferred_element_type=jnp.float32
            )
            for block in keys
        ]

    def attend(blocks, own=False):
        keys = [keys_of(block) for block in blocks]
        values = jnp.concatenate([piece for block in blocks for piece in values_of(block)], axis=1)
        ones = jnp.ones((ONES, values.shape[1]), jnp.bfloat16)
        values = jnp.concatenate([values, ones], axis=0)

        def finish(h, weight, alpha):
            part = jnp.dot(values, weight, preferred_element_type=jnp.float32)[: HD + 8]
            acc[h] = part if own else acc[h] * alpha + part

        ahead, behind = [scores(keys, h) for h in range(AHEAD)], None
        for h in range(heads):
            score = ahead.pop(0)
            if h + AHEAD < heads:
                ahead.append(scores(keys, h + AHEAD))
            if own:
                u = lax.broadcasted_iota(jnp.int32, (rows, rows), 0)
                t = lax.broadcasted_iota(jnp.int32, (rows, rows), 1)
                score = [jnp.where(u <= t, score[0], HIDE)]
            new, alpha = None, None
            for piece in score:
                most = jnp.max(piece, axis=0, keepdims=True)
                new = most if new is None else jnp.maximum(new, most)
            if not own:
                old = top[h : h + 1, :]
                new = jnp.maximum(old, new)
                alpha = jnp.exp2((old - new) * factor)
            weight = [jnp.exp2((piece - new) * factor).astype(jnp.bfloat16) for piece in score]
            top[h : h + 1, :] = new
            if behind is not None:
                finish(*behind)
            behind = (h, jnp.concatenate(weight, axis=0), alpha)
        finish(*behind)

    attend([me], own=True)

    def relay_up(hop, part):
        @pl.when(up_comes(hop, part))
        def _():
            arrived((chip - hop) * 2 + core, part)

            @pl.when(up_goes(hop, part))
            def _():
                up_copy(hop, part).start()

            side_copy(chip - hop, part).start()

    def relay_down(hop, part):
        source = lax.rem(chip + hop, CHIPS)

        def pass_on(stream):
            @pl.when(down_comes(hop, part, stream))
            def _():
                arrived(source * 2 + stream, part)

                @pl.when(down_goes(hop, part, stream))
                def _():
                    down_copy(hop, part, stream).start()

                @pl.when(down_hands(hop, part, stream))
                def _():
                    side_copy(source, part).start()

        pass_on(jnp.where(chip == 0, 0, core))

        @pl.when(chip == 0)
        def _():
            pass_on(1)

    def handed(block):
        for part in range(2):
            arrived(block, part)

    def one_round(hop, carry):
        below_source = jnp.where(chip == 0, 0, chip - hop)
        above_source = lax.rem(chip + hop, CHIPS)
        first = (chip == 1) | (chip == 5) | (chip == CHIPS - 1) | ((chip == CHIPS - 2) & (hop >= 3))

        @pl.when(hop >= 1)
        def _():
            for part in range(2):

                @pl.when(first)
                def _():
                    relay_down(hop, part)

                relay_up(hop, part)

                @pl.when(jnp.logical_not(first))
                def _():
                    relay_down(hop, part)

        pair = down_pair(hop)
        short = pair & (hop == 2) & (core == 1)
        doubles = jnp.where(short, 1, 2) * pair.astype(jnp.int32)
        alone = jnp.where(pair, 0, 2 * (chip >= hop).astype(jnp.int32))
        alone = jnp.where(short, 1, jnp.where(hop == 0, core, alone))
        alone = jnp.where(chip == 0, jnp.where(hop == 4, core, 0), alone)
        second = short | (hop == 0) | (chip == 0)

        def one_double(i, carry):
            @pl.when(i == 1)
            def _():
                handed(below_source * 2 + 1 - core)
                handed(above_source * 2 + 1 - core)

            side = jnp.where(i == 1, 1 - core, core)
            attend([below_source * 2 + side, above_source * 2 + side])
            return carry

        def one_block(i, carry):
            other = (i == 1) | second

            @pl.when(other)
            def _():
                handed(below_source * 2 + 1 - core)

            attend([below_source * 2 + jnp.where(other, 1 - core, core)])
            return carry

        lax.fori_loop(0, doubles, one_double, 0)
        lax.fori_loop(0, alone, one_block, 0)
        return carry

    lax.fori_loop(0, 5, one_round, 0)

    for h in range(heads):
        share = acc[h, 0:HD, :] * (1.0 / acc[h, HD : HD + 1, :])
        out_ref[:, h * HD : (h + 1) * HD] = share.astype(jnp.bfloat16).T

    for part in range(2):

        @pl.when(core == 0)
        def _():
            side_copy(chip, part).wait_send()

        def sent_up(hop, carry):
            up_copy(hop, part).wait_send()
            return carry

        def handed_over(hop, carry):
            side_copy(chip - hop, part).wait_send()
            return carry

        most = jnp.where(chip == CHIPS - 2, UP[part] - 1, 2)
        lax.fori_loop(0, jnp.where(chip == CHIPS - 1, 0, jnp.minimum(chip, most) + 1), sent_up, 0)
        most = jnp.where(chip == CHIPS - 1, UP[part], 3)
        lax.fori_loop(1, jnp.minimum(chip, most) + 1, handed_over, 0)

        for hop in range(4):
            stream = jnp.where((chip == 0) & (hop > 0), 0, core)

            @pl.when(down_goes(hop, part, stream))
            def _():
                down_copy(hop, part, stream).wait_send()

        @pl.when((chip == 0) & (core == 1))
        def _():
            for hop in range(1, 4):

                @pl.when(down_goes(hop, part, 1))
                def _():
                    down_copy(hop, part, 1).wait_send()

        @pl.when(chip >= 4)
        def _():
            for hop in range(2, 5):

                @pl.when(down_hands(hop, part, core))
                def _():
                    side_copy(lax.rem(chip + hop, CHIPS), part).wait_send()


def per_device(queries, keys, values, segment_ids):
    rows, width = queries.shape
    heads = width // HD
    size = 2 * rows + SEG
    operands = (queries, keys, values, segment_ids.reshape(rows // HD, HD))
    operands = [pltpu.with_memory_space_constraint(operand, pltpu.HBM) for operand in operands]
    return pl.pallas_call(
        kernel,
        out_shape=pltpu.VMEM((rows, width), jnp.bfloat16),
        in_specs=[pl.BlockSpec(memory_space=pltpu.HBM)] * 4,
        out_specs=pl.BlockSpec(memory_space=pltpu.VMEM),
        scratch_shapes=[
            pltpu.VMEM((2 * CHIPS, size, HD), jnp.bfloat16),
            pltpu.VMEM((rows, width), jnp.bfloat16),
            pltpu.VMEM((rows, HD), jnp.bfloat16),
            pltpu.VMEM((rows // HD, HD), jnp.int32),
            pltpu.VMEM((rows, HD), jnp.bfloat16),
            pltpu.VMEM((heads, rows), jnp.float32),
            pltpu.VMEM((heads, HD + 8, rows), jnp.float32),
            pltpu.SemaphoreType.DMA((4,)),
            pltpu.SemaphoreType.DMA((2 * CHIPS, 2)),
            pltpu.SemaphoreType.DMA((4, 2)),
            pltpu.SemaphoreType.DMA((4, 2, 2)),
            pltpu.SemaphoreType.DMA((CHIPS, 2)),
        ],
        compiler_params=pltpu.CompilerParams(
            collective_id=0, has_side_effects=True, vmem_limit_bytes=32 * 1024 * 1024
        ),
        cost_estimate=pl.CostEstimate(
            flops=4 * rows * rows * 13 * width,
            bytes_accessed=4 * rows * width,
            transcendentals=13 * rows * rows * heads,
        ),
        name="ring_attention",
    )(*operands)


def solution(mesh):
    in_specs = (
        P(("dp", "ctx"), "head"),
        P(("dp", "ctx"), "head"),
        P(("dp", "ctx"), "head"),
        P(("dp", "ctx")),
    )
    out_specs = P(("dp", "ctx"), "head")
    return jax.shard_map(
        per_device, mesh=mesh, in_specs=in_specs, out_specs=out_specs, check_vma=False
    )
```

```python
import functools
import math

import jax
import jax.numpy as jnp
from jax import lax
from jax.experimental import pallas as pl
from jax.experimental.pallas import tpu as pltpu
from jax.sharding import PartitionSpec as P

HD = 128
MESH = pl.DeviceIdType.MESH
CHIPS = 8
SEG = 16
ONES = 16
HIDE = -(2.0**30)
AHEAD = 2
UP = (4, 3)
DOWN = 4
LAST = (2, 3)


def kernel(
    q_ref, k_ref, v_ref, seg_ref, out_ref,
    kv, qv, vv, sv, qseg, top, acc,
    in_sem, recv_sem, up_sem, down_sem, side_sem,
):
    rows = k_ref.shape[0]
    heads = q_ref.shape[1] // HD
    factor = math.log2(math.e) * HD**-0.5
    me = lax.axis_index("ctx")
    chip, core = me // 2, me % 2
    sibling = chip * 2 + 1 - core
    above_chip, below_chip = lax.rem(chip + 1, CHIPS), lax.rem(chip + CHIPS - 1, CHIPS)

    def up_comes(hop, part):
        return (chip >= hop) & ((hop <= 3) | ((hop <= UP[part]) & (chip == CHIPS - 1)))

    def up_goes(hop, part):
        return (chip >= hop) & (chip < CHIPS - 1) & ((hop < 3) | ((hop < UP[part]) & (chip == CHIPS - 2)))

    def down_passes(stream):
        return jnp.where(chip == 0, core == 1, core == stream)

    def down_comes(hop, part, stream):
        here = (lax.rem(chip + hop, CHIPS) <= LAST[part]) & (hop >= 1) & (hop <= DOWN)
        return here & ((chip < CHIPS - 1) | (hop >= 2)) & down_passes(stream)

    def down_goes(hop, part, stream):
        own = (hop == 0) & (chip <= LAST[part]) & (core == stream)
        return own | (down_comes(hop, part, stream) & (hop < DOWN))

    def down_pair(hop):
        return (lax.rem(chip + hop, CHIPS) <= 2) & (chip >= 5) & (hop >= 2) & (hop <= 3)

    def down_hands(hop, part, stream):
        pair = down_pair(hop) & ((hop == 3) | (core == 1))
        return (pair | ((hop == 4) & (chip >= 4))) & down_comes(hop, part, stream)

    cuts = (pl.ds(0, rows), pl.ds(rows, SEG + rows))

    def remote(block, part, send, target):
        return pltpu.make_async_remote_copy(
            src_ref=kv.at[block, cuts[part]],
            dst_ref=kv.at[block, cuts[part]],
            send_sem=send,
            recv_sem=recv_sem.at[block, part],
            device_id={"ctx": target},
            device_id_type=MESH,
        )

    def up_copy(hop, part):
        return remote((chip - hop) * 2 + core, part, up_sem.at[hop, part], above_chip * 2 + core)

    def down_copy(hop, part, stream):
        block = lax.rem(chip + hop, CHIPS) * 2 + stream
        target = below_chip * 2 + jnp.where(chip == 1, 1, stream)
        target = jnp.where((chip == 0) & (hop == 0), (CHIPS - 2) * 2 + stream, target)
        return remote(block, part, down_sem.at[hop, part, stream], target)

    def side_copy(source, part):
        return remote(source * 2 + core, part, side_sem.at[source, part], sibling)

    def arrived(block, part):
        remote(block, part, side_sem.at[0, part], sibling).wait_recv()

    barrier = pltpu.get_barrier_semaphore()

    def greet(target):
        pl.semaphore_signal(barrier, inc=1, device_id={"ctx": target}, device_id_type=MESH)

    @pl.when(chip >= 1)
    def _():
        greet(below_chip * 2 + core)

    @pl.when((chip >= 1) & (chip != 3) & (chip < CHIPS - 1))
    def _():
        greet(above_chip * 2 + core)

    @pl.when(chip == CHIPS - 2)
    def _():
        greet(core)

    @pl.when(chip == CHIPS - 1)
    def _():
        greet(1)

    @pl.when((chip == 0) & (core == 1))
    def _():
        greet(2)
        greet(3)

    @pl.when((chip >= 1) | (core == 1))
    def _():
        greet(sibling)

    passer = (chip == 0) & (core == 1)
    partners = [chip < CHIPS - 1, chip != 4, passer, passer, (chip >= 1) | (core == 0)]

    k_in = pltpu.make_async_copy(k_ref, kv.at[me, pl.ds(0, rows)], in_sem.at[0])
    v_in = pltpu.make_async_copy(v_ref, vv, in_sem.at[1])
    q_in = pltpu.make_async_copy(q_ref, qv, in_sem.at[2])
    seg_in = pltpu.make_async_copy(seg_ref, sv, in_sem.at[3])
    k_in.start()
    seg_in.start()
    v_in.start()
    q_in.start()

    def send_own(part):
        @pl.when(chip <= 2)
        def _():
            down_copy(0, part, core).start()

        @pl.when(chip < CHIPS - 1)
        def _():
            up_copy(0, part).start()

        @pl.when((chip > 2) & (chip <= LAST[part]))
        def _():
            down_copy(0, part, core).start()

    k_in.wait()
    pl.semaphore_wait(barrier, sum(partner.astype(jnp.int32) for partner in partners))
    send_own(0)

    seg_in.wait()
    seg = sv[...]
    count = [
        jnp.sum(jnp.sum(jnp.where(seg <= d, 1.0, 0.0), axis=1, keepdims=True), axis=0, keepdims=True)
        for d in (0, 1)
    ]
    lane = lax.broadcasted_iota(jnp.int32, (8, HD), 1)
    low = jnp.where(lane == 1, count[0], jnp.where(lane == 2, count[1], 0.0))
    high = jnp.where(lane == 0, count[0], jnp.where(lane == 1, count[1], float(rows)))
    kv[me, rows : rows + SEG, :] = jnp.concatenate([low, high], axis=0).astype(jnp.bfloat16)
    v_in.wait()
    turned = vv[...].astype(jnp.float32).T.astype(jnp.bfloat16)
    for half in range(rows // HD):
        at = rows + SEG + half * HD
        kv[me, at : at + HD, :] = turned[:, half * HD : (half + 1) * HD]
    send_own(1)

    @pl.when(core == 0)
    def _():
        for part in range(2):
            side_copy(chip, part).start()

    def inside(low, high):
        place = lax.broadcasted_iota(jnp.int32, (rows, HD), 0).astype(jnp.float32)
        return (place >= low) & (place < high)

    lanes = lax.broadcasted_iota(jnp.int32, (rows, HD), 1)
    qseg[...] = jnp.where(inside(low[0:1], high[0:1]) & (lanes < 3), 1.0, 0.0).astype(jnp.bfloat16)
    q_in.wait()

    def keys_of(block):
        bounds = kv[block, rows : rows + SEG, :].astype(jnp.float32)
        hidden = jnp.where(inside(bounds[0:1], bounds[8:9]), 0.0, HIDE).astype(jnp.bfloat16)
        return jnp.concatenate([kv[block, 0:rows, :], hidden], axis=1)

    def values_of(block):
        first = rows + SEG
        return [kv[block, first + i * HD : first + (i + 1) * HD, :] for i in range(rows // HD)]

    def scores(keys, h):
        query = jnp.concatenate([qv[:, h * HD : (h + 1) * HD], qseg[...]], axis=1)
        return [
            lax.dot_general(
                block, query, (((1,), (1,)), ((), ())), preferred_element_type=jnp.float32
            )
            for block in keys
        ]

    def attend(blocks, own=False):
        keys = [keys_of(block) for block in blocks]
        values = jnp.concatenate([piece for block in blocks for piece in values_of(block)], axis=1)
        ones = jnp.ones((ONES, values.shape[1]), jnp.bfloat16)
        values = jnp.concatenate([values, ones], axis=0)

        def finish(h, weight, alpha):
            part = jnp.dot(values, weight, preferred_element_type=jnp.float32)[: HD + 8]
            acc[h] = part if own else acc[h] * alpha + part

        ahead, behind = [scores(keys, h) for h in range(AHEAD)], None
        for h in range(heads):
            score = ahead.pop(0)
            if h + AHEAD < heads:
                ahead.append(scores(keys, h + AHEAD))
            if own:
                u = lax.broadcasted_iota(jnp.int32, (rows, rows), 0)
                t = lax.broadcasted_iota(jnp.int32, (rows, rows), 1)
                score = [jnp.where(u <= t, score[0], HIDE)]
            new, alpha = None, None
            for piece in score:
                most = jnp.max(piece, axis=0, keepdims=True)
                new = most if new is None else jnp.maximum(new, most)
            if not own:
                old = top[h : h + 1, :]
                new = jnp.maximum(old, new)
                alpha = jnp.exp2((old - new) * factor)
            weight = [jnp.exp2((piece - new) * factor).astype(jnp.bfloat16) for piece in score]
            top[h : h + 1, :] = new
            if behind is not None:
                finish(*behind)
            behind = (h, jnp.concatenate(weight, axis=0), alpha)
        finish(*behind)

    attend([me], own=True)

    def relay_up(hop, part):
        @pl.when(up_comes(hop, part))
        def _():
            arrived((chip - hop) * 2 + core, part)

            @pl.when(up_goes(hop, part))
            def _():
                up_copy(hop, part).start()

            side_copy(chip - hop, part).start()

    def relay_down(hop, part):
        source = lax.rem(chip + hop, CHIPS)

        def pass_on(stream):
            @pl.when(down_comes(hop, part, stream))
            def _():
                arrived(source * 2 + stream, part)

                @pl.when(down_goes(hop, part, stream))
                def _():
                    down_copy(hop, part, stream).start()

                @pl.when(down_hands(hop, part, stream))
                def _():
                    side_copy(source, part).start()

        pass_on(jnp.where(chip == 0, 0, core))

        @pl.when(chip == 0)
        def _():
            pass_on(1)

    def handed(block):
        for part in range(2):
            arrived(block, part)

    def one_round(hop, carry):
        below_source = jnp.where(chip == 0, 0, chip - hop)
        above_source = lax.rem(chip + hop, CHIPS)
        first = (chip == 1) | (chip == 5) | (chip == CHIPS - 1) | ((chip == CHIPS - 2) & (hop >= 3))

        @pl.when(hop >= 1)
        def _():
            for part in range(2):

                @pl.when(first)
                def _():
                    relay_down(hop, part)

                relay_up(hop, part)

                @pl.when(jnp.logical_not(first))
                def _():
                    relay_down(hop, part)

        pair = down_pair(hop)
        short = pair & (hop == 2) & (core == 1)
        doubles = jnp.where(short, 1, 2) * pair.astype(jnp.int32)
        alone = jnp.where(pair, 0, 2 * (chip >= hop).astype(jnp.int32))
        alone = jnp.where(short, 1, jnp.where(hop == 0, 0, jnp.where(hop == 1, alone + core, alone)))
        alone = jnp.where(chip == 0, jnp.where(hop == 4, core, 0), alone)
        second = short | (hop == 0) | (chip == 0)

        def one_double(i, carry):
            @pl.when(i == 1)
            def _():
                handed(below_source * 2 + 1 - core)
                handed(above_source * 2 + 1 - core)

            side = jnp.where(i == 1, 1 - core, core)
            attend([below_source * 2 + side, above_source * 2 + side])
            return carry

        def one_block(i, carry):
            other = (i >= 1) | second
            source = jnp.where((hop == 1) & (i == 2), chip, below_source)

            @pl.when(other)
            def _():
                handed(source * 2 + 1 - core)

            attend([source * 2 + jnp.where(other, 1 - core, core)])
            return carry

        lax.fori_loop(0, doubles, one_double, 0)
        lax.fori_loop(0, alone, one_block, 0)
        return carry

    lax.fori_loop(0, 5, one_round, 0)

    for h in range(heads):
        share = acc[h, 0:HD, :] * (1.0 / acc[h, HD : HD + 1, :])
        out_ref[:, h * HD : (h + 1) * HD] = share.astype(jnp.bfloat16).T

    for part in range(2):

        @pl.when(core == 0)
        def _():
            side_copy(chip, part).wait_send()

        def sent_up(hop, carry):
            up_copy(hop, part).wait_send()
            return carry

        def handed_over(hop, carry):
            side_copy(chip - hop, part).wait_send()
            return carry

        most = jnp.where(chip == CHIPS - 2, UP[part] - 1, 2)
        lax.fori_loop(0, jnp.where(chip == CHIPS - 1, 0, jnp.minimum(chip, most) + 1), sent_up, 0)
        most = jnp.where(chip == CHIPS - 1, UP[part], 3)
        lax.fori_loop(1, jnp.minimum(chip, most) + 1, handed_over, 0)

        for hop in range(4):
            stream = jnp.where((chip == 0) & (hop > 0), 0, core)

            @pl.when(down_goes(hop, part, stream))
            def _():
                down_copy(hop, part, stream).wait_send()

        @pl.when((chip == 0) & (core == 1))
        def _():
            for hop in range(1, 4):

                @pl.when(down_goes(hop, part, 1))
                def _():
                    down_copy(hop, part, 1).wait_send()

        @pl.when(chip >= 4)
        def _():
            for hop in range(2, 5):

                @pl.when(down_hands(hop, part, core))
                def _():
                    side_copy(lax.rem(chip + hop, CHIPS), part).wait_send()


def per_device(queries, keys, values, segment_ids):
    rows, width = queries.shape
    heads = width // HD
    size = 2 * rows + SEG
    operands = (queries, keys, values, segment_ids.reshape(rows // HD, HD))
    operands = [pltpu.with_memory_space_constraint(operand, pltpu.HBM) for operand in operands]
    return pl.pallas_call(
        kernel,
        out_shape=pltpu.VMEM((rows, width), jnp.bfloat16),
        in_specs=[pl.BlockSpec(memory_space=pltpu.HBM)] * 4,
        out_specs=pl.BlockSpec(memory_space=pltpu.VMEM),
        scratch_shapes=[
            pltpu.VMEM((2 * CHIPS, size, HD), jnp.bfloat16),
            pltpu.VMEM((rows, width), jnp.bfloat16),
            pltpu.VMEM((rows, HD), jnp.bfloat16),
            pltpu.VMEM((rows // HD, HD), jnp.int32),
            pltpu.VMEM((rows, HD), jnp.bfloat16),
            pltpu.VMEM((heads, rows), jnp.float32),
            pltpu.VMEM((heads, HD + 8, rows), jnp.float32),
            pltpu.SemaphoreType.DMA((4,)),
            pltpu.SemaphoreType.DMA((2 * CHIPS, 2)),
            pltpu.SemaphoreType.DMA((4, 2)),
            pltpu.SemaphoreType.DMA((4, 2, 2)),
            pltpu.SemaphoreType.DMA((CHIPS, 2)),
        ],
        compiler_params=pltpu.CompilerParams(
            collective_id=0, has_side_effects=True, vmem_limit_bytes=32 * 1024 * 1024
        ),
        cost_estimate=pl.CostEstimate(
            flops=4 * rows * rows * 13 * width,
            bytes_accessed=4 * rows * width,
            transcendentals=13 * rows * rows * heads,
        ),
        name="ring_attention",
    )(*operands)


def solution(mesh):
    in_specs = (
        P(("dp", "ctx"), "head"),
        P(("dp", "ctx"), "head"),
        P(("dp", "ctx"), "head"),
        P(("dp", "ctx")),
    )
    out_specs = P(("dp", "ctx"), "head")
    return jax.shard_map(
        per_device, mesh=mesh, in_specs=in_specs, out_specs=out_specs, check_vma=False
    )
```
